256 devices in a mesh: lat: 8 (over y, x_lo), lon: 32 (over x_hi, z, core).
Axes of the slice: x: 4 (x_hi: 2, x_lo: 2; x = x_hi * 2 + x_lo), y: 4, z: 8, core: 2. Of those that a mesh axis runs over, the one named last changes fastest.
Arguments:
- input_field: bfloat16 [256, 2048, 256], P('lat', 'lon'), may hold values from -6 to 6
- cotangent: bfloat16 [256, 2048, 256], P('lat', 'lon'), may hold values from -6 to 6
- weight: bfloat16 [9, 256, 256], replicated, may hold values from -0.125 to 0.125
- basis_values: bfloat16 [256, 3, 65], replicated, may hold values from -3 to 3
- basis_index: int32 [256, 3, 65], replicated, may hold values from 0 to 9
- halo_width: int32 [256], replicated, may hold values from 1 to 32, as said below
Outputs:
- input_grad: float32 [256, 2048, 256], P('lat', 'lon')
- weight_grad: float32 [9, 256, 256], P(None, 'lat')
The draws below stay inside these ranges and needn't reach their ends.
Inputs may be any that keep to these rules, and one draw needn't show every extreme that they name: `basis_index`: value 9 marks an offset outside the filter's support. `halo_width`: rows 0 and 255 have width 32.
All inputs are finite; a program needn't handle non-finite values.
Results may differ from the reference program's by a relative error of at most 0.0042.
Values may be sent and summed in bfloat16 or wider, within the bound.
A program may use at most 192 MiB of HBM per device.

```python
import math
import jax
import jax.numpy as jnp
from jax import lax

C = 256
K = 9
HALO = 32
NLAT = 256
NLON = 2048


def draw_halo_width(key, part):
    key = jax.random.fold_in(key, 11)
    row_ids = jnp.arange(NLAT, dtype=jnp.int32)
    polar = jnp.minimum(row_ids, NLAT - 1 - row_ids)
    base_width = jnp.minimum(HALO, jnp.maximum(2, HALO * NLAT // (8 * (polar + 1))))
    jitter = jax.random.randint(key, (NLAT,), 0, 2, dtype=jnp.int32)
    jitter = jnp.where(polar > 0, jitter, 0)
    return jnp.maximum(1, base_width - jitter).astype(jnp.int32)


def with_ends(array, key, smallest, top_value):
    shape = array.shape
    place = [jax.random.randint(jax.random.fold_in(key, axis), (), 0, shape[axis]) for axis in range(len(shape))]
    array = array.at[tuple(place)].set(smallest)
    longest = shape.index(max(shape))
    place[longest] = (place[longest] + 1) % shape[longest]
    return array.at[tuple(place)].set(top_value)


def shard_levels(rng, extent, cuts, smallest, top_value):
    loudness = 1.0
    for dim, shards_of in cuts:
        heights = jax.random.uniform(jax.random.fold_in(jax.random.fold_in(rng, 6), dim), (shards_of,), jnp.float32, smallest / len(cuts), top_value / len(cuts))
        loudness = loudness * jnp.repeat(jnp.exp(heights), extent[dim] // shards_of).reshape((-1,) + (1,) * (len(extent) - 1 - dim))
    return loudness


def normal_values(rng, dims, scale, reach, cuts=(), held_as=jnp.bfloat16):
    gain = shard_levels(rng, dims, cuts, -0.22, 0.18) if cuts else 1.0
    result = jax.random.normal(rng, dims, jnp.float32) * scale * gain
    return jnp.minimum(jnp.maximum(result, -reach), reach).astype(held_as)


def setup_inputs(seed: int = 0) -> dict:
    seeds = jax.random.split(jax.random.key(seed), 7)
    return {
        "input_field": normal_values(seeds[0], (NLAT, NLON, C), 1.0, 6.0, ((0, 8), (1, 32))),
        "cotangent": normal_values(seeds[1], (NLAT, NLON, C), 1.0, 6.0, ((0, 8), (1, 32))),
        "weight": normal_values(seeds[2], (K, C, C), (K * C) ** -0.5, 0.125),
        "basis_values": normal_values(seeds[3], (NLAT, 3, 2 * HALO + 1), 0.5, 3.0),
        "basis_index": with_ends(jax.random.randint(seeds[4], (NLAT, 3, 2 * HALO + 1), 0, K + 1), jax.random.fold_in(seeds[4], 1), 0, K).astype(jnp.int32),
        "halo_width": draw_halo_width(jax.random.fold_in(seeds[6], 71), 0),
    }


def make_filter(basis_values, basis_index, halo_width):
    offsets = jnp.arange(2 * HALO + 1, dtype=jnp.int32) - HALO
    chosen = basis_index[:, None, :, :] == jnp.arange(K, dtype=jnp.int32)[None, :, None, None]
    inside = jnp.abs(offsets)[None, None, None, :] <= halo_width[:, None, None, None]
    zeros = jnp.zeros((), jnp.bfloat16)
    return jnp.where(chosen & inside, basis_values[:, None, :, :], zeros).astype(jnp.bfloat16)

def reference(input_field, cotangent, weight, basis_values, basis_index, halo_width):
    rows_f = jnp.arange(NLAT, dtype=jnp.int32).astype(jnp.float32)
    area_weight = jnp.pi / 2 * jnp.sin(jnp.pi * (rows_f + 0.5) / NLAT)
    filters = make_filter(basis_values, basis_index, halo_width)
    out_grad = (area_weight[:, None, None] * cotangent.astype(jnp.float32)).astype(jnp.bfloat16)
    padded = jnp.pad(input_field, ((1, 1), (0, 0), (0, 0)))
    offsets = jnp.arange(2 * HALO + 1, dtype=jnp.int32) - HALO
    positions = jnp.arange(NLON, dtype=jnp.int32)
    columns = (positions[None, :] + offsets[:, None]) % NLON
    inverse = (positions[None, :] - offsets[:, None]) % NLON
    taps = jnp.arange(2 * HALO + 1, dtype=jnp.int32)
    weight_f = weight.astype(jnp.float32)

    def row_step(carry, row_index):
        grad_acc, weight_acc = carry
        source_rows = lax.dynamic_slice_in_dim(padded, row_index, 3, 0)
        shifted = source_rows[:, columns, :]
        filter_row = filters[row_index].reshape(K, 3 * (2 * HALO + 1))
        basis_out = jnp.dot(filter_row, shifted.reshape(3 * (2 * HALO + 1), NLON * C), preferred_element_type=jnp.float32).astype(jnp.bfloat16)
        basis_out = basis_out.reshape(K, NLON, C)
        out_row = out_grad[row_index].astype(jnp.float32)
        weight_acc = weight_acc + jnp.einsum('kjc,jo->kco', basis_out.astype(jnp.float32), out_row)
        grad_basis = jnp.einsum('jo,kco->kjc', out_row, weight_f).astype(jnp.bfloat16)
        spread = jnp.dot(filter_row.T, grad_basis.reshape(K, NLON * C), preferred_element_type=jnp.float32)
        spread = spread.reshape(3, 2 * HALO + 1, NLON, C)
        gathered = spread[:, taps[:, None], inverse, :]
        returned_rows = lax.optimization_barrier(jnp.sum(gathered, axis=1))
        current = lax.dynamic_slice_in_dim(grad_acc, row_index, 3, 0)
        grad_acc = lax.dynamic_update_slice_in_dim(grad_acc, current + returned_rows, row_index, 0)
        return ((grad_acc, weight_acc), None)
    start_grad = jnp.zeros((NLAT + 2, NLON, C), jnp.float32)
    start_weight = jnp.zeros((K, C, C), jnp.float32)
    (grad_acc, weight_acc), unused = lax.scan(row_step, (start_grad, start_weight), jnp.arange(NLAT, dtype=jnp.int32))
    input_grad = grad_acc[1:-1]
    weight_grad = weight_acc / math.sqrt(NLAT * NLON)
    return (input_grad, weight_grad)
```

```python
import functools
import math

import jax
import jax.numpy as jnp
import numpy as np
from jax import lax
from jax.experimental import pallas as pl
from jax.experimental.pallas import tpu as pltpu
from jax.sharding import PartitionSpec as P

K = 9
HALO = 32
GROUP = 3
GROUPS = K // GROUP
WINDOW = 16
REACH = WINDOW + 2 * HALO
DEPTH = 3 * REACH
MESH = pl.DeviceIdType.MESH
BF16 = jnp.bfloat16
F32 = jnp.float32


def dot(a, b, dims):
    return lax.dot_general(a, b, (dims, ((), ())), preferred_element_type=F32)


def kernel(
    sizes,
    cot_hbm, field_hbm, weight_hbm, values_hbm, index_hbm, width_hbm, area_ref,
    grad_ref, wgrad_ref,
    cot, field, weight, values, index, width, flip_v, flip_i, taps, spread,
    part, pair, half, lat_in, band, lon_in, final,
    load_sems, halo_send, halo_recv, pair_send, pair_recv, lat_send, lat_recv,
    lon_send, lon_recv, all_send, all_recv, mate_send, mate_recv,
):
    n_lat, n_lon, rows, cols, chans, nlat, scale = sizes
    side_cols = cols // 2
    side_spots = rows * side_cols
    chips = n_lon // 2
    wide = chans // n_lat
    lanes = chans // 2
    lat = lax.axis_index("lat")
    lon = lax.axis_index("lon")
    core = lax.rem(lon, 2)
    chip = lax.div(lon, 2)
    has_up = lat > 0
    has_down = lat < n_lat - 1
    west = lax.rem(lon + n_lon - 1, n_lon)
    east = lax.rem(lon + 1, n_lon)
    mate = lon + 1 - 2 * core

    loads = [
        pltpu.make_async_copy(values_hbm, values, load_sems.at[0]),
        pltpu.make_async_copy(index_hbm, index, load_sems.at[1]),
        pltpu.make_async_copy(width_hbm, width, load_sems.at[2]),
        pltpu.make_async_copy(
            cot_hbm, cot.at[pl.ds(1, rows), pl.ds(HALO, cols)], load_sems.at[3]
        ),
        pltpu.make_async_copy(
            field_hbm.at[:, pl.ds(0, side_cols)], field.at[0], load_sems.at[4]
        ),
        pltpu.make_async_copy(
            field_hbm.at[:, pl.ds(side_cols, side_cols)], field.at[1], load_sems.at[5]
        ),
        pltpu.make_async_copy(weight_hbm, weight, load_sems.at[6]),
    ]
    for load in loads:
        load.start()

    barrier = pltpu.get_barrier_semaphore()

    def greet(device):
        pl.semaphore_signal(barrier, inc=1, device_id=device, device_id_type=MESH)

    def greet_corner(target):
        greet((target, west))
        greet((target, east))

    greet((lat, west))
    greet((lat, east))
    pl.when(has_up)(lambda: greet_corner(lat - 1))
    pl.when(has_down)(lambda: greet_corner(lat + 1))

    @pl.loop(1, n_lat)
    def _(step):
        greet((lax.rem(lat + step, n_lat), lon))

    @pl.loop(1, chips)
    def _(step):
        greet((lat, lax.rem(lon + 2 * step, n_lon)))

    corners = 2 * (has_up.astype(jnp.int32) + has_down.astype(jnp.int32))
    pl.semaphore_wait(barrier, n_lat - 1 + chips - 1 + 2 + corners)

    def halo(slot, source, target, device):
        return pltpu.make_async_remote_copy(
            src_ref=source, dst_ref=target,
            send_sem=halo_send.at[slot], recv_sem=halo_recv.at[slot],
            device_id=device, device_id_type=MESH,
        )

    low = pl.ds(0, HALO)
    high = pl.ds(cols - HALO, HALO)
    ext_low = pl.ds(0, HALO)
    ext_mid = pl.ds(HALO, cols)
    ext_high = pl.ds(cols + HALO, HALO)
    own_rows = pl.ds(1, rows)
    first, last = pl.ds(0, 1), pl.ds(rows - 1, 1)
    above, below = pl.ds(0, 1), pl.ds(rows + 1, 1)
    to_east = halo(0, cot_hbm.at[:, high], cot.at[own_rows, ext_low], (lat, east))
    to_west = halo(1, cot_hbm.at[:, low], cot.at[own_rows, ext_high], (lat, west))
    down = [
        halo(2, cot_hbm.at[last, high], cot.at[above, ext_low], (lat + 1, east)),
        halo(3, cot_hbm.at[last, low], cot.at[above, ext_high], (lat + 1, west)),
        halo(4, cot_hbm.at[last], cot.at[above, ext_mid], (lat + 1, lon)),
    ]
    up = [
        halo(5, cot_hbm.at[first, high], cot.at[below, ext_low], (lat - 1, east)),
        halo(6, cot_hbm.at[first, low], cot.at[below, ext_high], (lat - 1, west)),
        halo(7, cot_hbm.at[first], cot.at[below, ext_mid], (lat - 1, lon)),
    ]

    @pl.when(has_down)
    def _():
        for copy in down:
            copy.start()

    @pl.when(has_up)
    def _():
        for copy in up:
            copy.start()

    to_east.start()
    to_west.start()

    for load in loads[:3]:
        load.wait()
    size = 2 * HALO + 1
    tap_in = lax.broadcasted_iota(jnp.int32, (size, 128), 0)
    tap_out = lax.broadcasted_iota(jnp.int32, (size, 128), 1)
    reverse = jnp.where(tap_in + tap_out == 2 * HALO, 1.0, 0.0).astype(BF16)
    offset = jnp.abs(lax.broadcasted_iota(jnp.int32, (size, nlat), 0) - HALO)
    inside = offset <= width[...]
    for r in range(3):
        which = jnp.where(inside, index[r], K).astype(F32).astype(BF16)
        flip_v[r] = dot(values[r], reverse, ((0,), (0,)))
        flip_i[r] = dot(which, reverse, ((0,), (0,)))

    def clip_row(row):
        return jnp.clip(lat * rows + row - 1, 0, nlat - 1)

    @pl.loop(0, rows, unroll=8)
    def _(row):
        vals = jnp.zeros((WINDOW, 256), F32)
        which = jnp.zeros((WINDOW, 256), F32)
        rest = jnp.zeros((WINDOW, 128), F32)
        for t in range(3):
            at = pl.ds(clip_row(row + t), 1)
            spots = [
                jnp.concatenate(
                    [jnp.broadcast_to(table[2 - t, at, :], (WINDOW, 128)), rest], axis=1
                )
                for table in (flip_v, flip_i)
            ]
            spots = [pltpu.roll(x, REACH * t, 1, stride=1, stride_axis=0) for x in spots]
            vals += spots[0]
            which += spots[1]
        vals = vals.astype(BF16)
        which = which.astype(BF16)
        for k in range(K):
            taps[row, k * WINDOW : (k + 1) * WINDOW] = jnp.where(
                which == BF16(k), vals, jnp.zeros_like(vals)
            )

    def scale_rows(at, start, stop, columns):
        def body(row):
            factor = area_ref[clip_row(row)]
            cot[row, at] = (cot[row, at].astype(F32) * factor).astype(BF16)

        pl.loop(start, stop, unroll=4)(body)

    loads[3].wait()
    scale_rows(ext_mid, 1, rows + 1, cols)

    @pl.when(has_up)
    def _():
        for copy in down:
            copy.wait_recv()

    @pl.when(has_down)
    def _():
        for copy in up:
            copy.wait_recv()

    @pl.when(jnp.logical_not(has_up))
    def _():
        cot[0] = jnp.zeros_like(cot[0])

    @pl.when(jnp.logical_not(has_down))
    def _():
        cot[rows + 1] = jnp.zeros_like(cot[rows + 1])

    for edge in (0, rows + 1):
        cot[edge] = (cot[edge].astype(F32) * area_ref[clip_row(edge)]).astype(BF16)

    def filter_side(side):
        at = pl.ds(pl.multiple_of(side * (HALO + cols), HALO), HALO)

        def scale_row(row):
            factor = area_ref[clip_row(row)]
            cot[row, at] = (cot[row, at].astype(F32) * factor).astype(BF16)

        pl.loop(1, rows + 1, unroll=4)(scale_row)

        def filter_row(row):
            lhs = taps[row][:, :DEPTH]
            for u in range(side_cols // WINDOW):
                start = pl.multiple_of(side * side_cols + u * WINDOW, WINDOW)
                rhs = cot[pl.ds(row, 3), pl.ds(start, REACH)].reshape(DEPTH, chans)
                result = dot(lhs, rhs, ((1,), (0,))).astype(BF16)
                to = pl.ds(pl.multiple_of(row * side_cols + u * WINDOW, WINDOW), WINDOW)
                for k in range(K):
                    spread[side, k, to] = result[k * WINDOW : (k + 1) * WINDOW]

        pl.loop(0, rows, unroll=16)(filter_row)

    def field_product(side, k):
        lhs = field[side].reshape(side_spots, chans)
        return dot(lhs, spread[side, k], ((0,), (0,)))

    near = 1 - core
    far = core

    @pl.when(core == 0)
    def _():
        to_west.wait_recv()

    @pl.when(core == 1)
    def _():
        to_east.wait_recv()

    filter_side(near)
    loads[4].wait()
    loads[5].wait()
    for k in range(K):
        result = field_product(near, k)
        part[0, k] = result[:, :lanes]
        part[1, k] = result[:, lanes:]

    @pl.when(core == 0)
    def _():
        to_east.wait_recv()

    @pl.when(core == 1)
    def _():
        to_west.wait_recv()

    filter_side(far)

    def pair_copy(group):
        ks = pl.ds(group * GROUP, GROUP)
        return pltpu.make_async_remote_copy(
            src_ref=part.at[1 - core, ks], dst_ref=pair.at[ks],
            send_sem=pair_send.at[group], recv_sem=pair_recv.at[group],
            device_id=(lat, mate), device_id_type=MESH,
        )

    def lat_copy(group, step):
        ks = pl.ds(group * GROUP, GROUP)
        peer = lax.rem(lat + step, n_lat)
        return pltpu.make_async_remote_copy(
            src_ref=half.at[ks, pl.ds(pl.multiple_of(peer * wide, wide), wide)],
            dst_ref=lat_in.at[step, ks],
            send_sem=lat_send.at[group, step], recv_sem=lat_recv.at[group, step],
            device_id=(peer, lon), device_id_type=MESH,
        )

    def owner_of(k):
        return (k * chips) // K

    def lon_copy(k, step):
        return pltpu.make_async_remote_copy(
            src_ref=band.at[k], dst_ref=lon_in.at[step],
            send_sem=lon_send.at[k], recv_sem=lon_recv.at[step],
            device_id=(lat, owner_of(k) * 2 + core), device_id_type=MESH,
        )

    def reduce_pair(group):
        pair_copy(group).wait_recv()
        for k in range(group * GROUP, (group + 1) * GROUP):
            half[k] = (part[core, k] + pair[k]).astype(BF16)

        @pl.loop(1, n_lat)
        def _(step):
            lat_copy(group, step).start()

    def reduce_lat(group):
        @pl.loop(1, n_lat)
        def _(step):
            lat_copy(group, step).wait_recv()

        at = pl.ds(pl.multiple_of(lat * wide, wide), wide)
        for k in range(group * GROUP, (group + 1) * GROUP):
            total = half[k, at].astype(F32)
            for step in range(1, n_lat):
                total += lat_in[step, k].astype(F32)
            band[k] = total

            @pl.when(chip != owner_of(k))
            def _():
                lon_copy(k, lax.rem(owner_of(k) - chip + chips, chips)).start()

    for group in range(GROUPS):
        for k in range(group * GROUP, (group + 1) * GROUP):
            result = field_product(far, k)
            part[0, k] += result[:, :lanes]
            part[1, k] += result[:, lanes:]
        pair_copy(group).start()
        if group > 0:
            reduce_pair(group - 1)

    loads[6].wait()

    def grad_block(side, block):
        at = pl.ds(block * 256, 256)
        total = dot(spread[side, 0, at], weight[0], ((1,), (1,)))
        for k in range(1, K):
            total += dot(spread[side, k, at], weight[k], ((1,), (1,)))
        tall = 256 // side_cols
        to = pl.ds(block * tall, tall)
        grad_ref[to, side * side_cols : (side + 1) * side_cols] = total.reshape(
            tall, side_cols, chans
        )

    blocks = [(side, block) for side in range(2) for block in range(side_spots // 256)]
    share = -(-len(blocks) // 4)
    for block in blocks[:share]:
        grad_block(*block)
    reduce_pair(GROUPS - 1)
    for block in blocks[share : 2 * share]:
        grad_block(*block)
    reduce_lat(0)
    for block in blocks[2 * share : 3 * share]:
        grad_block(*block)
    reduce_lat(1)
    for block in blocks[3 * share :]:
        grad_block(*block)
    reduce_lat(2)

    def all_copy(k, step):
        return pltpu.make_async_remote_copy(
            src_ref=final.at[core, k], dst_ref=final.at[core, k],
            send_sem=all_send.at[step], recv_sem=all_recv.at[k],
            device_id=(lat, lax.rem(lon + 2 * step, n_lon)), device_id_type=MESH,
        )

    def mate_copy(k):
        return pltpu.make_async_remote_copy(
            src_ref=final.at[core, k], dst_ref=final.at[core, k],
            send_sem=mate_send.at[k], recv_sem=mate_recv.at[k],
            device_id=(lat, mate), device_id_type=MESH,
        )

    for k in range(K):
        @pl.when(chip == owner_of(k))
        def _():
            @pl.loop(1, chips)
            def _(step):
                lon_copy(k, step).wait_recv()

            total = band[k]
            for step in range(1, chips):
                total += lon_in[step]
            final[core, k] = (total * scale).astype(BF16)

            @pl.loop(1, chips)
            def _(step):
                all_copy(k, step).start()

            mate_copy(k).start()

    for k in range(K):
        @pl.when(chip != owner_of(k))
        def _():
            all_copy(k, 0).wait_recv()
            mate_copy(k).start()

    for k in range(K):
        mate_copy(k).wait_recv()
        for side in range(2):
            wgrad_ref[k, :, side * lanes : (side + 1) * lanes] = final[side, k].astype(F32)

    to_east.wait_send()
    to_west.wait_send()

    @pl.when(has_down)
    def _():
        for copy in down:
            copy.wait_send()

    @pl.when(has_up)
    def _():
        for copy in up:
            copy.wait_send()

    for group in range(GROUPS):
        pair_copy(group).wait_send()

        @pl.loop(1, n_lat)
        def _(step):
            lat_copy(group, step).wait_send()

    for k in range(K):
        mate_copy(k).wait_send()

        @pl.when(chip != owner_of(k))
        def _():
            lon_copy(k, 0).wait_send()

        @pl.when(chip == owner_of(k))
        def _():
            @pl.loop(1, chips)
            def _(step):
                all_copy(k, step).wait_send()


def shards(input_field, cotangent, weight, basis_values, basis_index, halo_width):
    n_lat = lax.axis_size("lat")
    n_lon = lax.axis_size("lon")
    rows, cols, chans = input_field.shape
    nlat = rows * n_lat
    chips = n_lon // 2
    wide = chans // n_lat
    lanes = chans // 2
    side_cols = cols // 2
    ext = cols + 2 * HALO
    size = 2 * HALO + 1
    centres = np.arange(nlat, dtype=np.float32) + np.float32(0.5)
    area = np.float32(np.pi / 2) * np.sin(np.float32(np.pi) * centres / np.float32(nlat))
    scale = 1.0 / math.sqrt(nlat * cols * n_lon)
    sizes = (n_lat, n_lon, rows, cols, chans, nlat, scale)
    whole = pl.BlockSpec(memory_space=pltpu.HBM)
    vmem = pl.BlockSpec(memory_space=pltpu.VMEM)
    smem = pl.BlockSpec(memory_space=pltpu.SMEM)
    dma = pltpu.SemaphoreType.DMA
    table = pltpu.VMEM((3, nlat, 128), F32)
    return pl.pallas_call(
        functools.partial(kernel, sizes),
        out_shape=(
            pltpu.VMEM((rows, cols, chans), F32),
            pltpu.VMEM((K, wide, chans), F32),
        ),
        in_specs=[whole] * 6 + [smem],
        out_specs=(vmem, vmem),
        scratch_shapes=[
            pltpu.VMEM((rows + 2, ext, chans), BF16),
            pltpu.VMEM((2, rows, side_cols, chans), BF16),
            pltpu.VMEM((K, chans, chans), BF16),
            pltpu.VMEM((3, size, nlat), BF16),
            pltpu.VMEM((3, size, nlat), jnp.int32),
            pltpu.VMEM((1, nlat), jnp.int32),
            table, table,
            pltpu.VMEM((rows, K * WINDOW, 256), BF16),
            pltpu.VMEM((2, K, rows * side_cols, chans), BF16),
            pltpu.VMEM((2, K, chans, lanes), F32),
            pltpu.VMEM((K, chans, lanes), F32),
            pltpu.VMEM((K, chans, lanes), BF16),
            pltpu.VMEM((n_lat, K, wide, lanes), BF16),
            pltpu.VMEM((K, wide, lanes), F32),
            pltpu.VMEM((chips, wide, lanes), F32),
            pltpu.VMEM((2, K, wide, lanes), BF16),
            dma((7,)), dma((8,)), dma((8,)), dma((GROUPS,)), dma((GROUPS,)),
            dma((GROUPS, n_lat)), dma((GROUPS, n_lat)), dma((K,)), dma((chips,)),
            dma((chips,)), dma((K,)), dma((K,)), dma((K,)),
        ],
        compiler_params=pltpu.CompilerParams(
            collective_id=0, has_side_effects=True, vmem_limit_bytes=40 * 2**20
        ),
        cost_estimate=pl.CostEstimate(
            flops=2 * K * rows * cols * chans * (3 * ext + 2 * chans),
            bytes_accessed=6 * 2**20, transcendentals=0,
        ),
    )(
        cotangent, input_field, weight,
        basis_values.transpose(1, 2, 0), basis_index.transpose(1, 2, 0),
        halo_width.reshape(1, nlat), jnp.asarray(area),
    )


def solution(mesh):
    in_specs = (P("lat", "lon", None), P("lat", "lon", None), P(), P(), P(), P())
    out_specs = (P("lat", "lon", None), P(None, "lat", None))
    return jax.shard_map(shards, mesh=mesh, in_specs=in_specs, out_specs=out_specs, check_vma=False)
```

```python
import functools
import math

import jax
import jax.numpy as jnp
from jax import lax
from jax.experimental import pallas as pl
from jax.experimental.pallas import tpu as pltpu
from jax.sharding import PartitionSpec as P

K = 9
HALO = 32
GROUP = 3
GROUPS = K // GROUP
WINDOW = 16
CHUNKS = 4
REACH = WINDOW + 2 * HALO
DEPTH = 3 * REACH
MESH = pl.DeviceIdType.MESH
BF16 = jnp.bfloat16
F32 = jnp.float32


def dot(a, b, dims):
    return lax.dot_general(a, b, (dims, ((), ())), preferred_element_type=F32)


def kernel(
    sizes,
    cot_hbm, field_hbm, weight_hbm, values_hbm, index_hbm, width_hbm,
    grad_ref, wgrad_ref,
    cot, field, weight, values, index, width, flip_v, flip_i, area, taps, spread,
    part, pair, half, lat_in, band, lon_in, final,
    load_sems, halo_send, halo_recv, pair_send, pair_recv, lat_send, lat_recv,
    lon_send, lon_recv, all_send, all_recv, mate_send, mate_recv,
):
    n_lat, n_lon, rows, cols, chans, nlat, scale = sizes
    side_cols = cols // 2
    side_spots = rows * side_cols
    chips = n_lon // 2
    wide = chans // n_lat
    lanes = chans // 2
    lat = lax.axis_index("lat")
    lon = lax.axis_index("lon")
    core = lax.rem(lon, 2)
    chip = lax.div(lon, 2)
    has_up = lat > 0
    has_down = lat < n_lat - 1
    west = lax.rem(lon + n_lon - 1, n_lon)
    east = lax.rem(lon + 1, n_lon)
    mate = lon + 1 - 2 * core

    loads = [
        pltpu.make_async_copy(values_hbm, values, load_sems.at[0]),
        pltpu.make_async_copy(index_hbm, index, load_sems.at[1]),
        pltpu.make_async_copy(width_hbm, width, load_sems.at[2]),
        pltpu.make_async_copy(
            cot_hbm, cot.at[pl.ds(1, rows), pl.ds(HALO, cols)], load_sems.at[3]
        ),
        pltpu.make_async_copy(
            field_hbm.at[:, pl.ds(0, side_cols)], field.at[0], load_sems.at[4]
        ),
        pltpu.make_async_copy(
            field_hbm.at[:, pl.ds(side_cols, side_cols)], field.at[1], load_sems.at[5]
        ),
        pltpu.make_async_copy(weight_hbm, weight, load_sems.at[6]),
    ]
    for load in loads:
        load.start()

    barrier = pltpu.get_barrier_semaphore()

    def greet(device):
        pl.semaphore_signal(barrier, inc=1, device_id=device, device_id_type=MESH)

    def greet_corner(target):
        greet((target, west))
        greet((target, east))

    greet((lat, west))
    greet((lat, east))
    pl.when(has_up)(lambda: greet_corner(lat - 1))
    pl.when(has_down)(lambda: greet_corner(lat + 1))

    @pl.loop(1, n_lat)
    def _(step):
        greet((lax.rem(lat + step, n_lat), lon))

    @pl.loop(1, chips)
    def _(step):
        greet((lat, lax.rem(lon + 2 * step, n_lon)))

    corners = 2 * (has_up.astype(jnp.int32) + has_down.astype(jnp.int32))
    pl.semaphore_wait(barrier, n_lat - 1 + chips - 1 + 2 + corners)

    def halo(slot, source, target, device):
        return pltpu.make_async_remote_copy(
            src_ref=source, dst_ref=target,
            send_sem=halo_send.at[slot], recv_sem=halo_recv.at[slot],
            device_id=device, device_id_type=MESH,
        )

    near = 1 - core
    far = core
    far_lon = lax.rem(lon + n_lon - 1 + 2 * core, n_lon)
    tall = rows // CHUNKS

    def columns(start, count):
        return pl.ds(pl.multiple_of(start, HALO), count)

    def far_copy(chunk, inward):
        side = far if inward else 1 - far
        return halo(
            chunk,
            cot_hbm.at[pl.ds(chunk * tall, tall), columns(core * (cols - HALO), HALO)],
            cot.at[pl.ds(1 + chunk * tall, tall), columns(side * (cols + HALO), HALO)],
            (lat, far_lon),
        )

    def near_copy(inward):
        side = near if inward else 1 - near
        return halo(
            CHUNKS,
            cot_hbm.at[:, columns((1 - core) * (cols - HALO), HALO)],
            cot.at[pl.ds(1, rows), columns(side * (cols + HALO), HALO)],
            (lat, mate),
        )

    low = pl.ds(0, HALO)
    high = pl.ds(cols - HALO, HALO)
    ext_low = pl.ds(0, HALO)
    ext_mid = pl.ds(HALO, cols)
    ext_high = pl.ds(cols + HALO, HALO)
    first, last = pl.ds(0, 1), pl.ds(rows - 1, 1)
    above, below = pl.ds(0, 1), pl.ds(rows + 1, 1)
    down = [
        halo(5, cot_hbm.at[last, high], cot.at[above, ext_low], (lat + 1, east)),
        halo(6, cot_hbm.at[last, low], cot.at[above, ext_high], (lat + 1, west)),
        halo(7, cot_hbm.at[last], cot.at[above, ext_mid], (lat + 1, lon)),
    ]
    up = [
        halo(8, cot_hbm.at[first, high], cot.at[below, ext_low], (lat - 1, east)),
        halo(9, cot_hbm.at[first, low], cot.at[below, ext_high], (lat - 1, west)),
        halo(10, cot_hbm.at[first], cot.at[below, ext_mid], (lat - 1, lon)),
    ]
    far_copy(0, False).start()
    near_copy(False).start()

    @pl.when(has_down)
    def _():
        for copy in down:
            copy.start()

    @pl.when(has_up)
    def _():
        for copy in up:
            copy.start()

    for chunk in range(1, CHUNKS):
        far_copy(chunk, False).start()

    latitude = lax.broadcasted_iota(jnp.int32, area.shape, 0) + (lat * rows - 1)
    area[...] = (math.pi / 2) * jnp.sin(math.pi * (latitude.astype(F32) + 0.5) / nlat)

    for load in loads[:3]:
        load.wait()
    size = 2 * HALO + 1
    tap_in = lax.broadcasted_iota(jnp.int32, (size, 128), 0)
    tap_out = lax.broadcasted_iota(jnp.int32, (size, 128), 1)
    reverse = jnp.where(tap_in + tap_out == 2 * HALO, 1.0, 0.0).astype(BF16)
    offset = jnp.abs(lax.broadcasted_iota(jnp.int32, (size, nlat), 0) - HALO)
    inside = offset <= width[...]
    for r in range(3):
        which = jnp.where(inside, index[r], K).astype(F32).astype(BF16)
        flip_v[r] = dot(values[r], reverse, ((0,), (0,)))
        flip_i[r] = dot(which, reverse, ((0,), (0,)))

    def clip_row(row):
        return jnp.clip(lat * rows + row - 1, 0, nlat - 1)

    @pl.loop(0, rows, unroll=8)
    def _(row):
        vals = jnp.zeros((WINDOW, 256), F32)
        which = jnp.zeros((WINDOW, 256), F32)
        rest = jnp.zeros((WINDOW, 128), F32)
        for t in range(3):
            at = pl.ds(clip_row(row + t), 1)
            spots = [
                jnp.concatenate(
                    [jnp.broadcast_to(table[2 - t, at, :], (WINDOW, 128)), rest], axis=1
                )
                for table in (flip_v, flip_i)
            ]
            spots = [pltpu.roll(x, REACH * t, 1, stride=1, stride_axis=0) for x in spots]
            vals += spots[0]
            which += spots[1]
        vals = vals.astype(BF16)
        which = which.astype(BF16)
        for k in range(K):
            taps[row, k * WINDOW : (k + 1) * WINDOW] = jnp.where(
                which == BF16(k), vals, jnp.zeros_like(vals)
            )

    def scale_row(row, at):
        factor = area[pl.ds(row, 1), :]
        factor = jnp.concatenate([factor] * (chans // 128), axis=1)
        cot[row, at] = (cot[row, at].astype(F32) * factor).astype(BF16)

    def scale_edge(row):
        scale_row(row, pl.ds(0, cols + 2 * HALO))

    loads[3].wait()
    pl.loop(1, rows + 1, unroll=4)(lambda row: scale_row(row, ext_mid))

    @pl.when(has_up)
    def _():
        for copy in down:
            copy.wait_recv()

    @pl.when(has_down)
    def _():
        for copy in up:
            copy.wait_recv()

    @pl.when(jnp.logical_not(has_up))
    def _():
        cot[0] = jnp.zeros_like(cot[0])

    @pl.when(jnp.logical_not(has_down))
    def _():
        cot[rows + 1] = jnp.zeros_like(cot[rows + 1])

    scale_edge(0)
    scale_edge(rows + 1)

    def filter_rows(side, start, stop):
        for row in range(start, stop):
            lhs = taps[row][:, :DEPTH]
            for u in range(side_cols // WINDOW):
                at = pl.ds(pl.multiple_of(side * side_cols + u * WINDOW, WINDOW), REACH)
                rhs = cot[row : row + 3, at].reshape(DEPTH, chans)
                result = dot(lhs, rhs, ((1,), (0,))).astype(BF16)
                to = row * side_cols + u * WINDOW
                for k in range(K):
                    spread[side, k, to : to + WINDOW] = result[k * WINDOW : (k + 1) * WINDOW]

    def field_product(side, k, start, stop):
        lhs = field[side, start:stop].reshape((stop - start) * side_cols, chans)
        rhs = spread[side, k, start * side_cols : stop * side_cols]
        return dot(lhs, rhs, ((0,), (0,)))

    def add_product(k, start, stop):
        result = field_product(far, k, start, stop)
        part[0, k] += result[:, :lanes]
        part[1, k] += result[:, lanes:]

    near_copy(True).wait_recv()
    near_at = columns(near * (cols + HALO), HALO)
    pl.loop(1, rows + 1, unroll=4)(lambda row: scale_row(row, near_at))
    filter_rows(near, 0, rows)
    loads[4].wait()
    loads[5].wait()
    for k in range(K):
        result = field_product(near, k, 0, rows)
        part[0, k] = result[:, :lanes]
        part[1, k] = result[:, lanes:]

    far_at = columns(far * (cols + HALO), HALO)
    for chunk in range(CHUNKS):
        if chunk == CHUNKS - 1:
            for k in range(K):
                add_product(k, 0, rows // 2)
        far_copy(chunk, True).wait_recv()
        for row in range(1 + chunk * tall, 1 + (chunk + 1) * tall):
            scale_row(row, far_at)
        start = chunk * tall - 1 if chunk else 0
        stop = (chunk + 1) * tall - 1 if chunk < CHUNKS - 1 else rows
        filter_rows(far, start, stop)

    def pair_copy(group):
        ks = pl.ds(group * GROUP, GROUP)
        return pltpu.make_async_remote_copy(
            src_ref=part.at[1 - core, ks], dst_ref=pair.at[ks],
            send_sem=pair_send.at[group], recv_sem=pair_recv.at[group],
            device_id=(lat, mate), device_id_type=MESH,
        )

    def lat_copy(group, step):
        ks = pl.ds(group * GROUP, GROUP)
        peer = lax.rem(lat + step, n_lat)
        return pltpu.make_async_remote_copy(
            src_ref=half.at[ks, pl.ds(pl.multiple_of(peer * wide, wide), wide)],
            dst_ref=lat_in.at[step, ks],
            send_sem=lat_send.at[group, step], recv_sem=lat_recv.at[group, step],
            device_id=(peer, lon), device_id_type=MESH,
        )

    def owner_of(k):
        return (k * chips) // K

    def lon_copy(k, step):
        return pltpu.make_async_remote_copy(
            src_ref=band.at[k], dst_ref=lon_in.at[step],
            send_sem=lon_send.at[k], recv_sem=lon_recv.at[step],
            device_id=(lat, owner_of(k) * 2 + core), device_id_type=MESH,
        )

    def reduce_pair(group):
        pair_copy(group).wait_recv()
        for k in range(group * GROUP, (group + 1) * GROUP):
            half[k] = (part[core, k] + pair[k]).astype(BF16)

        @pl.loop(1, n_lat)
        def _(step):
            lat_copy(group, step).start()

    def reduce_lat(group):
        @pl.loop(1, n_lat)
        def _(step):
            lat_copy(group, step).wait_recv()

        at = pl.ds(pl.multiple_of(lat * wide, wide), wide)
        for k in range(group * GROUP, (group + 1) * GROUP):
            total = half[k, at].astype(F32)
            for step in range(1, n_lat):
                total += lat_in[step, k].astype(F32)
            band[k] = total

            @pl.when(chip != owner_of(k))
            def _():
                lon_copy(k, lax.rem(owner_of(k) - chip + chips, chips)).start()

    for group in range(GROUPS):
        for k in range(group * GROUP, (group + 1) * GROUP):
            add_product(k, rows // 2, rows)
        pair_copy(group).start()

    loads[6].wait()

    def grad_block(side, block):
        at = pl.ds(block * 256, 256)
        total = dot(spread[side, 0, at], weight[0], ((1,), (1,)))
        for k in range(1, K):
            total += dot(spread[side, k, at], weight[k], ((1,), (1,)))
        high = 256 // side_cols
        to = pl.ds(block * high, high)
        grad_ref[to, side * side_cols : (side + 1) * side_cols] = total.reshape(
            high, side_cols, chans
        )

    blocks = [(side, block) for side in range(2) for block in range(side_spots // 256)]
    cuts = [len(blocks) * n // 8 for n in (0, 2, 3, 4, 8)]
    for step in range(4):
        for block in blocks[cuts[step] : cuts[step + 1]]:
            grad_block(*block)
        if step < GROUPS:
            reduce_pair(step)
    for group in range(GROUPS):
        reduce_lat(group)

    def all_copy(k, step):
        return pltpu.make_async_remote_copy(
            src_ref=final.at[core, k], dst_ref=final.at[core, k],
            send_sem=all_send.at[step], recv_sem=all_recv.at[k],
            device_id=(lat, lax.rem(lon + 2 * step, n_lon)), device_id_type=MESH,
        )

    def mate_copy(k):
        return pltpu.make_async_remote_copy(
            src_ref=final.at[core, k], dst_ref=final.at[core, k],
            send_sem=mate_send.at[k], recv_sem=mate_recv.at[k],
            device_id=(lat, mate), device_id_type=MESH,
        )

    for k in range(K):
        @pl.when(chip == owner_of(k))
        def _():
            @pl.loop(1, chips)
            def _(step):
                lon_copy(k, step).wait_recv()

            total = band[k]
            for step in range(1, chips):
                total += lon_in[step]
            final[core, k] = (total * scale).astype(BF16)

            @pl.loop(1, chips)
            def _(step):
                all_copy(k, step).start()

            mate_copy(k).start()

    for k in range(K):
        @pl.when(chip != owner_of(k))
        def _():
            all_copy(k, 0).wait_recv()
            mate_copy(k).start()

    for k in range(K):
        mate_copy(k).wait_recv()
        for side in range(2):
            wgrad_ref[k, :, side * lanes : (side + 1) * lanes] = final[side, k].astype(F32)

    near_copy(False).wait_send()
    for chunk in range(CHUNKS):
        far_copy(chunk, False).wait_send()

    @pl.when(has_down)
    def _():
        for copy in down:
            copy.wait_send()

    @pl.when(has_up)
    def _():
        for copy in up:
            copy.wait_send()

    for group in range(GROUPS):
        pair_copy(group).wait_send()

        @pl.loop(1, n_lat)
        def _(step):
            lat_copy(group, step).wait_send()

    for k in range(K):
        mate_copy(k).wait_send()

        @pl.when(chip != owner_of(k))
        def _():
            lon_copy(k, 0).wait_send()

        @pl.when(chip == owner_of(k))
        def _():
            @pl.loop(1, chips)
            def _(step):
                all_copy(k, step).wait_send()


def shards(input_field, cotangent, weight, basis_values, basis_index, halo_width):
    n_lat = lax.axis_size("lat")
    n_lon = lax.axis_size("lon")
    rows, cols, chans = input_field.shape
    nlat = rows * n_lat
    chips = n_lon // 2
    wide = chans // n_lat
    lanes = chans // 2
    side_cols = cols // 2
    ext = cols + 2 * HALO
    size = 2 * HALO + 1
    scale = 1.0 / math.sqrt(nlat * cols * n_lon)
    sizes = (n_lat, n_lon, rows, cols, chans, nlat, scale)
    whole = pl.BlockSpec(memory_space=pltpu.HBM)
    vmem = pl.BlockSpec(memory_space=pltpu.VMEM)
    dma = pltpu.SemaphoreType.DMA
    table = pltpu.VMEM((3, nlat, 128), F32)
    return pl.pallas_call(
        functools.partial(kernel, sizes),
        out_shape=(
            pltpu.VMEM((rows, cols, chans), F32),
            pltpu.VMEM((K, wide, chans), F32),
        ),
        in_specs=[whole] * 6,
        out_specs=(vmem, vmem),
        scratch_shapes=[
            pltpu.VMEM((rows + 2, ext, chans), BF16),
            pltpu.VMEM((2, rows, side_cols, chans), BF16),
            pltpu.VMEM((K, chans, chans), BF16),
            pltpu.VMEM((3, size, nlat), BF16),
            pltpu.VMEM((3, size, nlat), jnp.int32),
            pltpu.VMEM((1, nlat), jnp.int32),
            table, table,
            pltpu.VMEM((-(-(rows + 2) // 8) * 8, 128), F32),
            pltpu.VMEM((rows, K * WINDOW, 256), BF16),
            pltpu.VMEM((2, K, rows * side_cols, chans), BF16),
            pltpu.VMEM((2, K, chans, lanes), F32),
            pltpu.VMEM((K, chans, lanes), F32),
            pltpu.VMEM((K, chans, lanes), BF16),
            pltpu.VMEM((n_lat, K, wide, lanes), BF16),
            pltpu.VMEM((K, wide, lanes), F32),
            pltpu.VMEM((chips, wide, lanes), F32),
            pltpu.VMEM((2, K, wide, lanes), BF16),
            dma((7,)), dma((11,)), dma((11,)), dma((GROUPS,)), dma((GROUPS,)),
            dma((GROUPS, n_lat)), dma((GROUPS, n_lat)), dma((K,)), dma((chips,)),
            dma((chips,)), dma((K,)), dma((K,)), dma((K,)),
        ],
        compiler_params=pltpu.CompilerParams(
            collective_id=0, has_side_effects=True, vmem_limit_bytes=40 * 2**20
        ),
        cost_estimate=pl.CostEstimate(
            flops=2 * K * rows * cols * chans * (3 * ext + 2 * chans),
            bytes_accessed=6 * 2**20, transcendentals=0,
        ),
    )(
        *(
            pltpu.with_memory_space_constraint(x, pltpu.HBM) for x in (
            cotangent, input_field, weight,
            basis_values.transpose(1, 2, 0), basis_index.transpose(1, 2, 0),
            halo_width.reshape(1, nlat),
        )),
    )


def solution(mesh):
    in_specs = (P("lat", "lon", None), P("lat", "lon", None), P(), P(), P(), P())
    out_specs = (P("lat", "lon", None), P(None, "lat", None))
    return jax.shard_map(shards, mesh=mesh, in_specs=in_specs, out_specs=out_specs, check_vma=False)
```

```python
import functools
import math

import jax
import jax.numpy as jnp
from jax import lax
from jax.experimental import pallas as pl
from jax.experimental.pallas import tpu as pltpu
from jax.sharding import PartitionSpec as P

K = 9
HALO = 32
GROUP = 3
GROUPS = K // GROUP
WINDOW = 16
CHUNKS = 4
REACH = WINDOW + 2 * HALO
DEPTH = 3 * REACH
MESH = pl.DeviceIdType.MESH
BF16 = jnp.bfloat16
F32 = jnp.float32


def dot(a, b, dims):
    return lax.dot_general(a, b, (dims, ((), ())), preferred_element_type=F32)


def kernel(
    sizes,
    cot_hbm, field_hbm, weight_hbm, values_hbm, index_hbm, width_hbm,
    grad_ref, wgrad_ref,
    cot, field, weight, values, index, width, flip_v, flip_i, area, taps, spread,
    part, pair, half, lat_in, band, lon_in, final,
    load_sems, halo_send, halo_recv, pair_send, pair_recv, lat_send, lat_recv,
    lon_send, lon_recv, all_send, all_recv,
):
    n_lat, n_lon, rows, cols, chans, nlat, scale = sizes
    side_cols = cols // 2
    side_spots = rows * side_cols
    chips = n_lon // 2
    wide = chans // n_lat
    lanes = chans // 2
    ring = chips // 2
    lat = lax.axis_index("lat")
    lon = lax.axis_index("lon")
    core = lax.rem(lon, 2)
    chip = lax.div(lon, 2)
    spot = lax.rem(chip, ring)
    base = lon - lax.rem(lon, 2 * ring)
    has_up = lat > 0
    has_down = lat < n_lat - 1
    west = lax.rem(lon + n_lon - 1, n_lon)
    east = lax.rem(lon + 1, n_lon)
    mate = lon + 1 - 2 * core
    far_lon = lax.rem(lon + n_lon - 1 + 2 * core, n_lon)
    outside = jnp.logical_or(far_lon < base, far_lon >= base + 2 * ring)

    loads = [
        pltpu.make_async_copy(values_hbm, values, load_sems.at[0]),
        pltpu.make_async_copy(index_hbm, index, load_sems.at[1]),
        pltpu.make_async_copy(width_hbm, width, load_sems.at[2]),
        pltpu.make_async_copy(
            cot_hbm, cot.at[pl.ds(1, rows), pl.ds(HALO, cols)], load_sems.at[3]
        ),
        pltpu.make_async_copy(
            field_hbm.at[:, pl.ds(0, side_cols)], field.at[0], load_sems.at[4]
        ),
        pltpu.make_async_copy(
            field_hbm.at[:, pl.ds(side_cols, side_cols)], field.at[1], load_sems.at[5]
        ),
        pltpu.make_async_copy(weight_hbm, weight, load_sems.at[6]),
    ]
    for load in loads:
        load.start()

    barrier = pltpu.get_barrier_semaphore()

    def greet(device):
        pl.semaphore_signal(barrier, inc=1, device_id=device, device_id_type=MESH)

    def greet_corner(target):
        greet((target, west))
        greet((target, east))

    pl.when(outside)(lambda: greet((lat, far_lon)))
    pl.when(has_up)(lambda: greet_corner(lat - 1))
    pl.when(has_down)(lambda: greet_corner(lat + 1))

    @pl.loop(1, n_lat)
    def _(step):
        greet((lax.rem(lat + step, n_lat), lon))

    @pl.loop(1, chips)
    def _(step):
        greet((lat, lax.rem(lon + 2 * step, n_lon)))

    @pl.loop(0, ring)
    def _(step):
        greet((lat, base + lax.rem(mate - base + 2 * step, 2 * ring)))

    corners = 2 * (has_up.astype(jnp.int32) + has_down.astype(jnp.int32))
    others = n_lat - 1 + chips - 1 + ring + outside.astype(jnp.int32)
    pl.semaphore_wait(barrier, others + corners)

    def halo(slot, source, target, device):
        return pltpu.make_async_remote_copy(
            src_ref=source, dst_ref=target,
            send_sem=halo_send.at[slot], recv_sem=halo_recv.at[slot],
            device_id=device, device_id_type=MESH,
        )

    near = 1 - core
    far = core
    tall = rows // CHUNKS

    def columns(start, count):
        return pl.ds(pl.multiple_of(start, HALO), count)

    def far_copy(chunk, inward):
        side = far if inward else 1 - far
        return halo(
            chunk,
            cot_hbm.at[pl.ds(chunk * tall, tall), columns(core * (cols - HALO), HALO)],
            cot.at[pl.ds(1 + chunk * tall, tall), columns(side * (cols + HALO), HALO)],
            (lat, far_lon),
        )

    def near_copy(inward):
        side = near if inward else 1 - near
        return halo(
            CHUNKS,
            cot_hbm.at[:, columns((1 - core) * (cols - HALO), HALO)],
            cot.at[pl.ds(1, rows), columns(side * (cols + HALO), HALO)],
            (lat, mate),
        )

    low = pl.ds(0, HALO)
    high = pl.ds(cols - HALO, HALO)
    ext_low = pl.ds(0, HALO)
    ext_mid = pl.ds(HALO, cols)
    ext_high = pl.ds(cols + HALO, HALO)
    first, last = pl.ds(0, 1), pl.ds(rows - 1, 1)
    above, below = pl.ds(0, 1), pl.ds(rows + 1, 1)
    down = [
        halo(5, cot_hbm.at[last, high], cot.at[above, ext_low], (lat + 1, east)),
        halo(6, cot_hbm.at[last, low], cot.at[above, ext_high], (lat + 1, west)),
        halo(7, cot_hbm.at[last], cot.at[above, ext_mid], (lat + 1, lon)),
    ]
    up = [
        halo(8, cot_hbm.at[first, high], cot.at[below, ext_low], (lat - 1, east)),
        halo(9, cot_hbm.at[first, low], cot.at[below, ext_high], (lat - 1, west)),
        halo(10, cot_hbm.at[first], cot.at[below, ext_mid], (lat - 1, lon)),
    ]
    far_copy(0, False).start()

    @pl.when(has_down)
    def _():
        for copy in down:
            copy.start()

    @pl.when(has_up)
    def _():
        for copy in up:
            copy.start()

    near_copy(False).start()
    for chunk in range(1, CHUNKS):
        far_copy(chunk, False).start()

    latitude = lax.broadcasted_iota(jnp.int32, area.shape, 0) + (lat * rows - 1)
    area[...] = (math.pi / 2) * jnp.sin(math.pi * (latitude.astype(F32) + 0.5) / nlat)

    for load in loads[:3]:
        load.wait()
    size = 2 * HALO + 1
    tap_in = lax.broadcasted_iota(jnp.int32, (size, 128), 0)
    tap_out = lax.broadcasted_iota(jnp.int32, (size, 128), 1)
    reverse = jnp.where(tap_in + tap_out == 2 * HALO, 1.0, 0.0).astype(BF16)
    offset = jnp.abs(lax.broadcasted_iota(jnp.int32, (size, nlat), 0) - HALO)
    inside = offset <= width[...]
    for r in range(3):
        which = jnp.where(inside, index[r], K).astype(F32).astype(BF16)
        flip_v[r] = dot(values[r], reverse, ((0,), (0,)))
        flip_i[r] = dot(which, reverse, ((0,), (0,)))

    def clip_row(row):
        return jnp.clip(lat * rows + row - 1, 0, nlat - 1)

    @pl.loop(0, rows, unroll=8)
    def _(row):
        vals = jnp.zeros((WINDOW, 256), F32)
        which = jnp.zeros((WINDOW, 256), F32)
        rest = jnp.zeros((WINDOW, 128), F32)
        for t in range(3):
            at = pl.ds(clip_row(row + t), 1)
            spots = [
                jnp.concatenate(
                    [jnp.broadcast_to(table[2 - t, at, :], (WINDOW, 128)), rest], axis=1
                )
                for table in (flip_v, flip_i)
            ]
            spots = [pltpu.roll(x, REACH * t, 1, stride=1, stride_axis=0) for x in spots]
            vals += spots[0]
            which += spots[1]
        vals = vals.astype(BF16)
        which = which.astype(BF16)
        for k in range(K):
            taps[row, k * WINDOW : (k + 1) * WINDOW] = jnp.where(
                which == BF16(k), vals, jnp.zeros_like(vals)
            )

    def scale_row(row, at):
        factor = area[pl.ds(row, 1), :]
        factor = jnp.concatenate([factor] * (chans // 128), axis=1)
        cot[row, at] = (cot[row, at].astype(F32) * factor).astype(BF16)

    def scale_edge(row):
        scale_row(row, pl.ds(0, cols + 2 * HALO))

    loads[3].wait()
    pl.loop(1, rows + 1, unroll=4)(lambda row: scale_row(row, ext_mid))

    def filter_rows(side, start, stop):
        for row in range(start, stop):
            lhs = taps[row][:, :DEPTH]
            for u in range(side_cols // WINDOW):
                at = pl.ds(pl.multiple_of(side * side_cols + u * WINDOW, WINDOW), REACH)
                rhs = cot[row : row + 3, at].reshape(DEPTH, chans)
                result = dot(lhs, rhs, ((1,), (0,))).astype(BF16)
                to = row * side_cols + u * WINDOW
                for k in range(K):
                    spread[side, k, to : to + WINDOW] = result[k * WINDOW : (k + 1) * WINDOW]

    def field_product(side, k, start, stop):
        lhs = field[side, start:stop].reshape((stop - start) * side_cols, chans)
        rhs = spread[side, k, start * side_cols : stop * side_cols]
        return dot(lhs, rhs, ((0,), (0,)))

    def add_product(k, start, stop):
        result = field_product(far, k, start, stop)
        part[0, k] += result[:, :lanes]
        part[1, k] += result[:, lanes:]

    near_copy(True).wait_recv()
    near_at = columns(near * (cols + HALO), HALO)
    pl.loop(1, rows + 1, unroll=4)(lambda row: scale_row(row, near_at))
    filter_rows(near, 1, rows - 1)

    @pl.when(has_up)
    def _():
        for copy in down:
            copy.wait_recv()

    @pl.when(has_down)
    def _():
        for copy in up:
            copy.wait_recv()

    @pl.when(jnp.logical_not(has_up))
    def _():
        cot[0] = jnp.zeros_like(cot[0])

    @pl.when(jnp.logical_not(has_down))
    def _():
        cot[rows + 1] = jnp.zeros_like(cot[rows + 1])

    scale_edge(0)
    scale_edge(rows + 1)
    filter_rows(near, 0, 1)
    filter_rows(near, rows - 1, rows)
    loads[4].wait()
    loads[5].wait()
    for k in range(K):
        result = field_product(near, k, 0, rows)
        part[0, k] = result[:, :lanes]
        part[1, k] = result[:, lanes:]

    far_at = columns(far * (cols + HALO), HALO)
    for chunk in range(CHUNKS):
        if chunk == CHUNKS - 1:
            for k in range(K):
                add_product(k, 0, rows // 2)
        far_copy(chunk, True).wait_recv()
        for row in range(1 + chunk * tall, 1 + (chunk + 1) * tall):
            scale_row(row, far_at)
        start = chunk * tall - 1 if chunk else 0
        stop = (chunk + 1) * tall - 1 if chunk < CHUNKS - 1 else rows
        filter_rows(far, start, stop)

    def pair_copy(group):
        ks = pl.ds(group * GROUP, GROUP)
        return pltpu.make_async_remote_copy(
            src_ref=part.at[1 - core, ks], dst_ref=pair.at[ks],
            send_sem=pair_send.at[group], recv_sem=pair_recv.at[group],
            device_id=(lat, mate), device_id_type=MESH,
        )

    def lat_copy(group, step):
        ks = pl.ds(group * GROUP, GROUP)
        peer = lax.rem(lat + step, n_lat)
        return pltpu.make_async_remote_copy(
            src_ref=half.at[ks, pl.ds(pl.multiple_of(peer * wide, wide), wide)],
            dst_ref=lat_in.at[step, ks],
            send_sem=lat_send.at[group, step], recv_sem=lat_recv.at[group, step],
            device_id=(peer, lon), device_id_type=MESH,
        )

    def lon_copy(k, half_ring):
        owner = half_ring * ring + k % ring
        return owner, pltpu.make_async_remote_copy(
            src_ref=band.at[k], dst_ref=lon_in.at[k // ring, chip],
            send_sem=lon_send.at[k, half_ring], recv_sem=lon_recv.at[k // ring, chip],
            device_id=(lat, owner * 2 + core), device_id_type=MESH,
        )

    def lon_arrival(k, source):
        return pltpu.make_async_remote_copy(
            src_ref=band.at[k], dst_ref=lon_in.at[k // ring, source],
            send_sem=lon_send.at[k, 0], recv_sem=lon_recv.at[k // ring, source],
            device_id=(lat, source * 2 + core), device_id_type=MESH,
        )

    def reduce_pair(group):
        pair_copy(group).wait_recv()
        for k in range(group * GROUP, (group + 1) * GROUP):
            half[k] = (part[core, k] + pair[k]).astype(BF16)

        @pl.loop(1, n_lat)
        def _(step):
            lat_copy(group, step).start()

    def reduce_lat(group):
        @pl.loop(1, n_lat)
        def _(step):
            lat_copy(group, step).wait_recv()

        at = pl.ds(pl.multiple_of(lat * wide, wide), wide)
        for k in range(group * GROUP, (group + 1) * GROUP):
            total = half[k, at].astype(F32)
            for step in range(1, n_lat):
                total += lat_in[step, k].astype(F32)
            band[k] = total.astype(BF16)
            for half_ring in range(2):
                owner, copy = lon_copy(k, half_ring)
                pl.when(chip != owner)(copy.start)

    for group in range(GROUPS):
        for k in range(group * GROUP, (group + 1) * GROUP):
            add_product(k, rows // 2, rows)
        pair_copy(group).start()

    loads[6].wait()

    def grad_block(side, block):
        at = pl.ds(block * 256, 256)
        total = dot(spread[side, 0, at], weight[0], ((1,), (1,)))
        for k in range(1, K):
            total += dot(spread[side, k, at], weight[k], ((1,), (1,)))
        high = 256 // side_cols
        to = pl.ds(block * high, high)
        grad_ref[to, side * side_cols : (side + 1) * side_cols] = total.reshape(
            high, side_cols, chans
        )

    blocks = [(side, block) for side in range(2) for block in range(side_spots // 256)]
    cuts = [len(blocks) * n // 8 for n in (0, 2, 3, 4, 8)]
    for step in range(4):
        for block in blocks[cuts[step] : cuts[step + 1]]:
            grad_block(*block)
        if step < GROUPS:
            reduce_pair(step)
    for group in range(GROUPS):
        reduce_lat(group)

    def all_copy(k, step):
        return pltpu.make_async_remote_copy(
            src_ref=final.at[core, k], dst_ref=final.at[core, k],
            send_sem=all_send.at[k // ring, step], recv_sem=all_recv.at[core, k],
            device_id=(lat, base + lax.rem(lon - base + step, 2 * ring)),
            device_id_type=MESH,
        )

    def all_arrival(k, half_core):
        return pltpu.make_async_remote_copy(
            src_ref=final.at[half_core, k], dst_ref=final.at[half_core, k],
            send_sem=all_send.at[0, 0], recv_sem=all_recv.at[half_core, k],
            device_id=(lat, base + 2 * (k % ring) + half_core), device_id_type=MESH,
        )

    for k in range(K):
        @pl.when(spot == k % ring)
        def _():
            @pl.loop(1, chips)
            def _(step):
                lon_arrival(k, lax.rem(chip + step, chips)).wait_recv()

            total = band[k].astype(F32)
            for step in range(1, chips):
                total += lon_in[k // ring, lax.rem(chip + step, chips)].astype(F32)
            final[core, k] = (total * scale).astype(BF16)

            @pl.loop(1, 2 * ring)
            def _(step):
                all_copy(k, step).start()

    for k in range(K):
        for half_core in range(2):
            @pl.when(jnp.logical_or(spot != k % ring, core != half_core))
            def _():
                all_arrival(k, half_core).wait_recv()

            of_core = slice(half_core * lanes, (half_core + 1) * lanes)
            wgrad_ref[k, :, of_core] = final[half_core, k].astype(F32)

    near_copy(False).wait_send()
    for chunk in range(CHUNKS):
        far_copy(chunk, False).wait_send()

    @pl.when(has_down)
    def _():
        for copy in down:
            copy.wait_send()

    @pl.when(has_up)
    def _():
        for copy in up:
            copy.wait_send()

    for group in range(GROUPS):
        pair_copy(group).wait_send()

        @pl.loop(1, n_lat)
        def _(step):
            lat_copy(group, step).wait_send()

    for k in range(K):
        for half_ring in range(2):
            owner, copy = lon_copy(k, half_ring)
            pl.when(chip != owner)(copy.wait_send)

        @pl.when(spot == k % ring)
        def _():
            @pl.loop(1, 2 * ring)
            def _(step):
                all_copy(k, step).wait_send()


def shards(input_field, cotangent, weight, basis_values, basis_index, halo_width):
    n_lat = lax.axis_size("lat")
    n_lon = lax.axis_size("lon")
    rows, cols, chans = input_field.shape
    nlat = rows * n_lat
    chips = n_lon // 2
    wide = chans // n_lat
    lanes = chans // 2
    ring = chips // 2
    held = -(-K // ring)
    side_cols = cols // 2
    ext = cols + 2 * HALO
    size = 2 * HALO + 1
    scale = 1.0 / math.sqrt(nlat * cols * n_lon)
    sizes = (n_lat, n_lon, rows, cols, chans, nlat, scale)
    whole = pl.BlockSpec(memory_space=pltpu.HBM)
    vmem = pl.BlockSpec(memory_space=pltpu.VMEM)
    dma = pltpu.SemaphoreType.DMA
    table = pltpu.VMEM((3, nlat, 128), F32)
    return pl.pallas_call(
        functools.partial(kernel, sizes),
        out_shape=(
            pltpu.VMEM((rows, cols, chans), F32),
            pltpu.VMEM((K, wide, chans), F32),
        ),
        in_specs=[whole] * 6,
        out_specs=(vmem, vmem),
        scratch_shapes=[
            pltpu.VMEM((rows + 2, ext, chans), BF16),
            pltpu.VMEM((2, rows, side_cols, chans), BF16),
            pltpu.VMEM((K, chans, chans), BF16),
            pltpu.VMEM((3, size, nlat), BF16),
            pltpu.VMEM((3, size, nlat), jnp.int32),
            pltpu.VMEM((1, nlat), jnp.int32),
            table, table,
            pltpu.VMEM((-(-(rows + 2) // 8) * 8, 128), F32),
            pltpu.VMEM((rows, K * WINDOW, 256), BF16),
            pltpu.VMEM((2, K, rows * side_cols, chans), BF16),
            pltpu.VMEM((2, K, chans, lanes), F32),
            pltpu.VMEM((K, chans, lanes), F32),
            pltpu.VMEM((K, chans, lanes), BF16),
            pltpu.VMEM((n_lat, K, wide, lanes), BF16),
            pltpu.VMEM((K, wide, lanes), BF16),
            pltpu.VMEM((held, chips, wide, lanes), BF16),
            pltpu.VMEM((2, K, wide, lanes), BF16),
            dma((7,)), dma((11,)), dma((11,)), dma((GROUPS,)), dma((GROUPS,)),
            dma((GROUPS, n_lat)), dma((GROUPS, n_lat)), dma((K, 2)), dma((held, chips)),
            dma((held, 2 * ring)), dma((2, K)),
        ],
        compiler_params=pltpu.CompilerParams(
            collective_id=0, has_side_effects=True, vmem_limit_bytes=40 * 2**20
        ),
        cost_estimate=pl.CostEstimate(
            flops=2 * K * rows * cols * chans * (3 * ext + 2 * chans),
            bytes_accessed=6 * 2**20, transcendentals=0,
        ),
    )(
        *(
            pltpu.with_memory_space_constraint(x, pltpu.HBM) for x in (
            cotangent, input_field, weight,
            basis_values.transpose(1, 2, 0), basis_index.transpose(1, 2, 0),
            halo_width.reshape(1, nlat),
        )),
    )


def solution(mesh):
    in_specs = (P("lat", "lon", None), P("lat", "lon", None), P(), P(), P(), P())
    out_specs = (P("lat", "lon", None), P(None, "lat", None))
    return jax.shard_map(shards, mesh=mesh, in_specs=in_specs, out_specs=out_specs, check_vma=False)
```

```python
import functools
import math

import jax
import jax.numpy as jnp
from jax import lax
from jax.experimental import pallas as pl
from jax.experimental.pallas import tpu as pltpu
from jax.sharding import PartitionSpec as P

K = 9
HALO = 32
GROUP = 3
GROUPS = K // GROUP
WINDOW = 16
CHUNKS = 4
REACH = WINDOW + 2 * HALO
DEPTH = 3 * REACH
MESH = pl.DeviceIdType.MESH
BF16 = jnp.bfloat16
F32 = jnp.float32


def dot(a, b, dims):
    return lax.dot_general(a, b, (dims, ((), ())), preferred_element_type=F32)


def kernel(
    sizes,
    cot_hbm, field_hbm, weight_hbm, values_hbm, index_hbm, width_hbm,
    grad_ref, wgrad_ref,
    cot, field, weight, values, index, width, flip_v, flip_i, area, taps, spread,
    part, pair, half, lat_in, band, lon_in, final,
    load_sems, halo_send, halo_recv, pair_send, pair_recv, lat_send, lat_recv,
    lon_send, lon_recv, all_send, all_recv,
):
    n_lat, n_lon, rows, cols, chans, nlat, scale = sizes
    side_cols = cols // 2
    side_spots = rows * side_cols
    chips = n_lon // 2
    wide = chans // n_lat
    lanes = chans // 2
    ring = chips // 2
    lat = lax.axis_index("lat")
    lon = lax.axis_index("lon")
    core = lax.rem(lon, 2)
    chip = lax.div(lon, 2)
    spot = lax.rem(chip, ring)
    base = lon - lax.rem(lon, 2 * ring)
    has_up = lat > 0
    has_down = lat < n_lat - 1
    west = lax.rem(lon + n_lon - 1, n_lon)
    east = lax.rem(lon + 1, n_lon)
    mate = lon + 1 - 2 * core
    far_lon = lax.rem(lon + n_lon - 1 + 2 * core, n_lon)
    outside = jnp.logical_or(far_lon < base, far_lon >= base + 2 * ring)

    loads = [
        pltpu.make_async_copy(values_hbm, values, load_sems.at[0]),
        pltpu.make_async_copy(index_hbm, index, load_sems.at[1]),
        pltpu.make_async_copy(width_hbm, width, load_sems.at[2]),
        pltpu.make_async_copy(
            cot_hbm, cot.at[pl.ds(1, rows), pl.ds(HALO, cols)], load_sems.at[3]
        ),
        pltpu.make_async_copy(
            field_hbm.at[:, pl.ds(0, side_cols)], field.at[0], load_sems.at[4]
        ),
        pltpu.make_async_copy(
            field_hbm.at[:, pl.ds(side_cols, side_cols)], field.at[1], load_sems.at[5]
        ),
        pltpu.make_async_copy(weight_hbm, weight, load_sems.at[6]),
    ]
    for load in loads:
        load.start()

    barrier = pltpu.get_barrier_semaphore()

    def greet(device):
        pl.semaphore_signal(barrier, inc=1, device_id=device, device_id_type=MESH)

    def greet_corner(target):
        greet((target, west))
        greet((target, east))

    pl.when(outside)(lambda: greet((lat, far_lon)))
    pl.when(has_up)(lambda: greet_corner(lat - 1))
    pl.when(has_down)(lambda: greet_corner(lat + 1))

    @pl.loop(1, n_lat)
    def _(step):
        greet((lax.rem(lat + step, n_lat), lon))

    @pl.loop(1, chips)
    def _(step):
        greet((lat, lax.rem(lon + 2 * step, n_lon)))

    @pl.loop(0, ring)
    def _(step):
        greet((lat, base + lax.rem(mate - base + 2 * step, 2 * ring)))

    corners = 2 * (has_up.astype(jnp.int32) + has_down.astype(jnp.int32))
    others = n_lat - 1 + chips - 1 + ring + outside.astype(jnp.int32)
    pl.semaphore_wait(barrier, others + corners)

    def halo(slot, source, target, device):
        return pltpu.make_async_remote_copy(
            src_ref=source, dst_ref=target,
            send_sem=halo_send.at[slot], recv_sem=halo_recv.at[slot],
            device_id=device, device_id_type=MESH,
        )

    near = 1 - core
    far = core
    tall = rows // CHUNKS

    def columns(start, count):
        return pl.ds(pl.multiple_of(start, HALO), count)

    def far_copy(chunk, inward):
        side = far if inward else 1 - far
        return halo(
            chunk,
            cot_hbm.at[pl.ds(chunk * tall, tall), columns(core * (cols - HALO), HALO)],
            cot.at[pl.ds(1 + chunk * tall, tall), columns(side * (cols + HALO), HALO)],
            (lat, far_lon),
        )

    def near_copy(inward):
        side = near if inward else 1 - near
        return halo(
            CHUNKS,
            cot_hbm.at[:, columns((1 - core) * (cols - HALO), HALO)],
            cot.at[pl.ds(1, rows), columns(side * (cols + HALO), HALO)],
            (lat, mate),
        )

    low = pl.ds(0, HALO)
    high = pl.ds(cols - HALO, HALO)
    ext_low = pl.ds(0, HALO)
    ext_mid = pl.ds(HALO, cols)
    ext_high = pl.ds(cols + HALO, HALO)
    first, last = pl.ds(0, 1), pl.ds(rows - 1, 1)
    above, below = pl.ds(0, 1), pl.ds(rows + 1, 1)
    down = [
        halo(5, cot_hbm.at[last, high], cot.at[above, ext_low], (lat + 1, east)),
        halo(6, cot_hbm.at[last, low], cot.at[above, ext_high], (lat + 1, west)),
        halo(7, cot_hbm.at[last], cot.at[above, ext_mid], (lat + 1, lon)),
    ]
    up = [
        halo(8, cot_hbm.at[first, high], cot.at[below, ext_low], (lat - 1, east)),
        halo(9, cot_hbm.at[first, low], cot.at[below, ext_high], (lat - 1, west)),
        halo(10, cot_hbm.at[first], cot.at[below, ext_mid], (lat - 1, lon)),
    ]

    @pl.when(has_down)
    def _():
        for copy in down:
            copy.start()

    @pl.when(has_up)
    def _():
        for copy in up:
            copy.start()

    near_copy(False).start()
    for chunk in range(CHUNKS):
        far_copy(chunk, False).start()

    latitude = lax.broadcasted_iota(jnp.int32, area.shape, 0) + (lat * rows - 1)
    area[...] = (math.pi / 2) * jnp.sin(math.pi * (latitude.astype(F32) + 0.5) / nlat)

    for load in loads[:3]:
        load.wait()
    size = 2 * HALO + 1
    tap_in = lax.broadcasted_iota(jnp.int32, (size, 128), 0)
    tap_out = lax.broadcasted_iota(jnp.int32, (size, 128), 1)
    reverse = jnp.where(tap_in + tap_out == 2 * HALO, 1.0, 0.0).astype(BF16)
    offset = jnp.abs(lax.broadcasted_iota(jnp.int32, (size, nlat), 0) - HALO)
    inside = offset <= width[...]
    for r in range(3):
        which = jnp.where(inside, index[r], K).astype(F32).astype(BF16)
        flip_v[r] = dot(values[r], reverse, ((0,), (0,)))
        flip_i[r] = dot(which, reverse, ((0,), (0,)))

    def clip_row(row):
        return jnp.clip(lat * rows + row - 1, 0, nlat - 1)

    @pl.loop(0, rows, unroll=8)
    def _(row):
        vals = jnp.zeros((WINDOW, 256), F32)
        which = jnp.zeros((WINDOW, 256), F32)
        rest = jnp.zeros((WINDOW, 128), F32)
        for t in range(3):
            at = pl.ds(clip_row(row + t), 1)
            spots = [
                jnp.concatenate(
                    [jnp.broadcast_to(table[2 - t, at, :], (WINDOW, 128)), rest], axis=1
                )
                for table in (flip_v, flip_i)
            ]
            spots = [pltpu.roll(x, REACH * t, 1, stride=1, stride_axis=0) for x in spots]
            vals += spots[0]
            which += spots[1]
        vals = vals.astype(BF16)
        which = which.astype(BF16)
        for k in range(K):
            taps[row, k * WINDOW : (k + 1) * WINDOW] = jnp.where(
                which == BF16(k), vals, jnp.zeros_like(vals)
            )

    def scale_row(row, at):
        factor = area[pl.ds(row, 1), :]
        factor = jnp.concatenate([factor] * (chans // 128), axis=1)
        cot[row, at] = (cot[row, at].astype(F32) * factor).astype(BF16)

    def scale_edge(row):
        scale_row(row, pl.ds(0, cols + 2 * HALO))

    loads[3].wait()
    pl.loop(1, rows + 1, unroll=4)(lambda row: scale_row(row, ext_mid))

    def filter_rows(side, start, stop):
        for row in range(start, stop):
            lhs = taps[row][:, :DEPTH]
            for u in range(side_cols // WINDOW):
                at = pl.ds(pl.multiple_of(side * side_cols + u * WINDOW, WINDOW), REACH)
                rhs = cot[row : row + 3, at].reshape(DEPTH, chans)
                result = dot(lhs, rhs, ((1,), (0,))).astype(BF16)
                to = row * side_cols + u * WINDOW
                for k in range(K):
                    spread[side, k, to : to + WINDOW] = result[k * WINDOW : (k + 1) * WINDOW]

    def field_product(side, k, start, stop):
        lhs = field[side, start:stop].reshape((stop - start) * side_cols, chans)
        rhs = spread[side, k, start * side_cols : stop * side_cols]
        return dot(lhs, rhs, ((0,), (0,)))

    def add_product(k, start, stop):
        result = field_product(far, k, start, stop)
        part[0, k] += result[:, :lanes]
        part[1, k] += result[:, lanes:]

    near_copy(True).wait_recv()
    near_at = columns(near * (cols + HALO), HALO)
    pl.loop(1, rows + 1, unroll=4)(lambda row: scale_row(row, near_at))
    filter_rows(near, 1, rows - 1)

    loads[4].wait()
    loads[5].wait()
    for k in range(K):
        result = field_product(near, k, 1, rows - 1)
        part[0, k] = result[:, :lanes]
        part[1, k] = result[:, lanes:]

    far_at = columns(far * (cols + HALO), HALO)
    for chunk in range(CHUNKS):
        if chunk == CHUNKS - 1:
            for k in range(K):
                add_product(k, 1, rows // 2)
        far_copy(chunk, True).wait_recv()
        for row in range(1 + chunk * tall, 1 + (chunk + 1) * tall):
            scale_row(row, far_at)
        start = max(chunk * tall - 1, 1)
        stop = (chunk + 1) * tall - 1
        filter_rows(far, start, stop)

    @pl.when(has_up)
    def _():
        for copy in down:
            copy.wait_recv()

    @pl.when(has_down)
    def _():
        for copy in up:
            copy.wait_recv()

    @pl.when(jnp.logical_not(has_up))
    def _():
        cot[0] = jnp.zeros_like(cot[0])

    @pl.when(jnp.logical_not(has_down))
    def _():
        cot[rows + 1] = jnp.zeros_like(cot[rows + 1])

    scale_edge(0)
    scale_edge(rows + 1)
    for side in range(2):
        filter_rows(side, 0, 1)
        filter_rows(side, rows - 1, rows)

    def add_edges(k):
        ends = (0, rows - 1)
        lhs = jnp.concatenate([field[side, row] for side in range(2) for row in ends], axis=0)
        rhs = jnp.concatenate(
            [
                spread[side, k, row * side_cols : (row + 1) * side_cols]
                for side in range(2)
                for row in ends
            ],
            axis=0,
        )
        result = dot(lhs, rhs, ((0,), (0,)))
        part[0, k] += result[:, :lanes]
        part[1, k] += result[:, lanes:]

    def pair_copy(group):
        ks = pl.ds(group * GROUP, GROUP)
        return pltpu.make_async_remote_copy(
            src_ref=part.at[1 - core, ks], dst_ref=pair.at[ks],
            send_sem=pair_send.at[group], recv_sem=pair_recv.at[group],
            device_id=(lat, mate), device_id_type=MESH,
        )

    def lat_copy(group, step):
        ks = pl.ds(group * GROUP, GROUP)
        peer = lax.rem(lat + step, n_lat)
        return pltpu.make_async_remote_copy(
            src_ref=half.at[ks, pl.ds(pl.multiple_of(peer * wide, wide), wide)],
            dst_ref=lat_in.at[step, ks],
            send_sem=lat_send.at[group, step], recv_sem=lat_recv.at[group, step],
            device_id=(peer, lon), device_id_type=MESH,
        )

    def lon_copy(k, half_ring):
        owner = half_ring * ring + k % ring
        return owner, pltpu.make_async_remote_copy(
            src_ref=band.at[k], dst_ref=lon_in.at[k // ring, chip],
            send_sem=lon_send.at[k, half_ring], recv_sem=lon_recv.at[k // ring, chip],
            device_id=(lat, owner * 2 + core), device_id_type=MESH,
        )

    def lon_arrival(k, source):
        return pltpu.make_async_remote_copy(
            src_ref=band.at[k], dst_ref=lon_in.at[k // ring, source],
            send_sem=lon_send.at[k, 0], recv_sem=lon_recv.at[k // ring, source],
            device_id=(lat, source * 2 + core), device_id_type=MESH,
        )

    def reduce_pair(group):
        pair_copy(group).wait_recv()
        for k in range(group * GROUP, (group + 1) * GROUP):
            half[k] = (part[core, k] + pair[k]).astype(BF16)

        @pl.loop(1, n_lat)
        def _(step):
            lat_copy(group, step).start()

    def reduce_lat(group):
        @pl.loop(1, n_lat)
        def _(step):
            lat_copy(group, step).wait_recv()

        at = pl.ds(pl.multiple_of(lat * wide, wide), wide)
        for k in range(group * GROUP, (group + 1) * GROUP):
            total = half[k, at].astype(F32)
            for step in range(1, n_lat):
                total += lat_in[step, k].astype(F32)
            band[k] = total.astype(BF16)
            for half_ring in range(2):
                owner, copy = lon_copy(k, half_ring)
                pl.when(chip != owner)(copy.start)

    for group in range(GROUPS):
        for k in range(group * GROUP, (group + 1) * GROUP):
            add_product(k, rows // 2, rows - 1)
            add_edges(k)
        pair_copy(group).start()

    loads[6].wait()

    def grad_block(side, block):
        at = pl.ds(block * 256, 256)
        total = dot(spread[side, 0, at], weight[0], ((1,), (1,)))
        for k in range(1, K):
            total += dot(spread[side, k, at], weight[k], ((1,), (1,)))
        high = 256 // side_cols
        to = pl.ds(block * high, high)
        grad_ref[to, side * side_cols : (side + 1) * side_cols] = total.reshape(
            high, side_cols, chans
        )

    blocks = [(side, block) for side in range(2) for block in range(side_spots // 256)]
    cuts = [len(blocks) * n // 8 for n in (0, 2, 3, 4, 8)]
    for step in range(4):
        for block in blocks[cuts[step] : cuts[step + 1]]:
            grad_block(*block)
        if step < GROUPS:
            reduce_pair(step)
    for group in range(GROUPS):
        reduce_lat(group)

    def all_copy(k, step):
        return pltpu.make_async_remote_copy(
            src_ref=final.at[core, k], dst_ref=final.at[core, k],
            send_sem=all_send.at[k // ring, step], recv_sem=all_recv.at[core, k],
            device_id=(lat, base + lax.rem(lon - base + step, 2 * ring)),
            device_id_type=MESH,
        )

    def all_arrival(k, half_core):
        return pltpu.make_async_remote_copy(
            src_ref=final.at[half_core, k], dst_ref=final.at[half_core, k],
            send_sem=all_send.at[0, 0], recv_sem=all_recv.at[half_core, k],
            device_id=(lat, base + 2 * (k % ring) + half_core), device_id_type=MESH,
        )

    for k in range(K):
        @pl.when(spot == k % ring)
        def _():
            @pl.loop(1, chips)
            def _(step):
                lon_arrival(k, lax.rem(chip + step, chips)).wait_recv()

            total = band[k].astype(F32)
            for step in range(1, chips):
                total += lon_in[k // ring, lax.rem(chip + step, chips)].astype(F32)
            final[core, k] = (total * scale).astype(BF16)

            @pl.loop(1, 2 * ring)
            def _(step):
                all_copy(k, step).start()

    for k in range(K):
        for half_core in range(2):
            @pl.when(jnp.logical_or(spot != k % ring, core != half_core))
            def _():
                all_arrival(k, half_core).wait_recv()

            of_core = slice(half_core * lanes, (half_core + 1) * lanes)
            wgrad_ref[k, :, of_core] = final[half_core, k].astype(F32)

    near_copy(False).wait_send()
    for chunk in range(CHUNKS):
        far_copy(chunk, False).wait_send()

    @pl.when(has_down)
    def _():
        for copy in down:
            copy.wait_send()

    @pl.when(has_up)
    def _():
        for copy in up:
            copy.wait_send()

    for group in range(GROUPS):
        pair_copy(group).wait_send()

        @pl.loop(1, n_lat)
        def _(step):
            lat_copy(group, step).wait_send()

    for k in range(K):
        for half_ring in range(2):
            owner, copy = lon_copy(k, half_ring)
            pl.when(chip != owner)(copy.wait_send)

        @pl.when(spot == k % ring)
        def _():
            @pl.loop(1, 2 * ring)
            def _(step):
                all_copy(k, step).wait_send()


def shards(input_field, cotangent, weight, basis_values, basis_index, halo_width):
    n_lat = lax.axis_size("lat")
    n_lon = lax.axis_size("lon")
    rows, cols, chans = input_field.shape
    nlat = rows * n_lat
    chips = n_lon // 2
    wide = chans // n_lat
    lanes = chans // 2
    ring = chips // 2
    held = -(-K // ring)
    side_cols = cols // 2
    ext = cols + 2 * HALO
    size = 2 * HALO + 1
    scale = 1.0 / math.sqrt(nlat * cols * n_lon)
    sizes = (n_lat, n_lon, rows, cols, chans, nlat, scale)
    whole = pl.BlockSpec(memory_space=pltpu.HBM)
    vmem = pl.BlockSpec(memory_space=pltpu.VMEM)
    dma = pltpu.SemaphoreType.DMA
    table = pltpu.VMEM((3, nlat, 128), F32)
    return pl.pallas_call(
        functools.partial(kernel, sizes),
        out_shape=(
            pltpu.VMEM((rows, cols, chans), F32),
            pltpu.VMEM((K, wide, chans), F32),
        ),
        in_specs=[whole] * 6,
        out_specs=(vmem, vmem),
        scratch_shapes=[
            pltpu.VMEM((rows + 2, ext, chans), BF16),
            pltpu.VMEM((2, rows, side_cols, chans), BF16),
            pltpu.VMEM((K, chans, chans), BF16),
            pltpu.VMEM((3, size, nlat), BF16),
            pltpu.VMEM((3, size, nlat), jnp.int32),
            pltpu.VMEM((1, nlat), jnp.int32),
            table, table,
            pltpu.VMEM((-(-(rows + 2) // 8) * 8, 128), F32),
            pltpu.VMEM((rows, K * WINDOW, 256), BF16),
            pltpu.VMEM((2, K, rows * side_cols, chans), BF16),
            pltpu.VMEM((2, K, chans, lanes), F32),
            pltpu.VMEM((K, chans, lanes), F32),
            pltpu.VMEM((K, chans, lanes), BF16),
            pltpu.VMEM((n_lat, K, wide, lanes), BF16),
            pltpu.VMEM((K, wide, lanes), BF16),
            pltpu.VMEM((held, chips, wide, lanes), BF16),
            pltpu.VMEM((2, K, wide, lanes), BF16),
            dma((7,)), dma((11,)), dma((11,)), dma((GROUPS,)), dma((GROUPS,)),
            dma((GROUPS, n_lat)), dma((GROUPS, n_lat)), dma((K, 2)), dma((held, chips)),
            dma((held, 2 * ring)), dma((2, K)),
        ],
        compiler_params=pltpu.CompilerParams(
            collective_id=0, has_side_effects=True, vmem_limit_bytes=40 * 2**20
        ),
        cost_estimate=pl.CostEstimate(
            flops=2 * K * rows * cols * chans * (3 * ext + 2 * chans),
            bytes_accessed=6 * 2**20, transcendentals=0,
        ),
    )(
        *(
            pltpu.with_memory_space_constraint(x, pltpu.HBM) for x in (
            cotangent, input_field, weight,
            basis_values.transpose(1, 2, 0), basis_index.transpose(1, 2, 0),
            halo_width.reshape(1, nlat),
        )),
    )


def solution(mesh):
    in_specs = (P("lat", "lon", None), P("lat", "lon", None), P(), P(), P(), P())
    out_specs = (P("lat", "lon", None), P(None, "lat", None))
    return jax.shard_map(shards, mesh=mesh, in_specs=in_specs, out_specs=out_specs, check_vma=False)
```

```python
import functools
import math

import jax
import jax.numpy as jnp
from jax import lax
from jax.experimental import pallas as pl
from jax.experimental.pallas import tpu as pltpu
from jax.sharding import PartitionSpec as P

K = 9
HALO = 32
GROUP = 3
GROUPS = K // GROUP
WINDOW = 16
CHUNKS = 4
REACH = WINDOW + 2 * HALO
DEPTH = 3 * REACH
MESH = pl.DeviceIdType.MESH
BF16 = jnp.bfloat16
F32 = jnp.float32


def dot(a, b, dims):
    return lax.dot_general(a, b, (dims, ((), ())), preferred_element_type=F32)


def kernel(
    sizes,
    cot_hbm, field_hbm, weight_hbm, values_hbm, index_hbm, width_hbm,
    grad_ref, wgrad_ref,
    cot, field, weight, values, index, width, flip_v, flip_i, area, taps, spread,
    part, pair, half, lat_in, band, lon_in, final,
    load_sems, halo_send, halo_recv, pair_send, pair_recv, lat_send, lat_recv,
    lon_send, lon_recv, all_send, all_recv,
):
    n_lat, n_lon, rows, cols, chans, nlat, scale = sizes
    side_cols = cols // 2
    side_spots = rows * side_cols
    chips = n_lon // 2
    wide = chans // n_lat
    lanes = chans // 2
    ring = chips // 2
    lat = lax.axis_index("lat")
    lon = lax.axis_index("lon")
    core = lax.rem(lon, 2)
    chip = lax.div(lon, 2)
    spot = lax.rem(chip, ring)
    base = lon - lax.rem(lon, 2 * ring)
    has_up = lat > 0
    has_down = lat < n_lat - 1
    west = lax.rem(lon + n_lon - 1, n_lon)
    east = lax.rem(lon + 1, n_lon)
    mate = lon + 1 - 2 * core
    far_lon = lax.rem(lon + n_lon - 1 + 2 * core, n_lon)
    outside = jnp.logical_or(far_lon < base, far_lon >= base + 2 * ring)

    loads = [
        pltpu.make_async_copy(values_hbm, values, load_sems.at[0]),
        pltpu.make_async_copy(index_hbm, index, load_sems.at[1]),
        pltpu.make_async_copy(width_hbm, width, load_sems.at[2]),
        pltpu.make_async_copy(
            cot_hbm, cot.at[pl.ds(1, rows), pl.ds(HALO, cols)], load_sems.at[3]
        ),
        pltpu.make_async_copy(
            field_hbm.at[:, pl.ds(0, side_cols)], field.at[0], load_sems.at[4]
        ),
        pltpu.make_async_copy(
            field_hbm.at[:, pl.ds(side_cols, side_cols)], field.at[1], load_sems.at[5]
        ),
        pltpu.make_async_copy(weight_hbm, weight, load_sems.at[6]),
    ]
    for load in loads:
        load.start()

    barrier = pltpu.get_barrier_semaphore()

    def greet(device):
        pl.semaphore_signal(barrier, inc=1, device_id=device, device_id_type=MESH)

    def greet_corner(target):
        greet((target, west))
        greet((target, east))

    pl.when(outside)(lambda: greet((lat, far_lon)))
    pl.when(has_up)(lambda: greet_corner(lat - 1))
    pl.when(has_down)(lambda: greet_corner(lat + 1))

    @pl.loop(1, n_lat)
    def _(step):
        greet((lax.rem(lat + step, n_lat), lon))

    @pl.loop(1, chips)
    def _(step):
        greet((lat, lax.rem(lon + 2 * step, n_lon)))

    @pl.loop(0, ring)
    def _(step):
        greet((lat, base + lax.rem(mate - base + 2 * step, 2 * ring)))

    corners = 2 * (has_up.astype(jnp.int32) + has_down.astype(jnp.int32))
    others = n_lat - 1 + chips - 1 + ring + outside.astype(jnp.int32)
    pl.semaphore_wait(barrier, others + corners)

    def halo(slot, source, target, device):
        return pltpu.make_async_remote_copy(
            src_ref=source, dst_ref=target,
            send_sem=halo_send.at[slot], recv_sem=halo_recv.at[slot],
            device_id=device, device_id_type=MESH,
        )

    near = 1 - core
    far = core
    tall = rows // CHUNKS

    def columns(start, count):
        return pl.ds(pl.multiple_of(start, HALO), count)

    def far_copy(chunk, inward):
        side = far if inward else 1 - far
        return halo(
            chunk,
            cot_hbm.at[pl.ds(chunk * tall, tall), columns(core * (cols - HALO), HALO)],
            cot.at[pl.ds(1 + chunk * tall, tall), columns(side * (cols + HALO), HALO)],
            (lat, far_lon),
        )

    def near_copy(inward):
        side = near if inward else 1 - near
        return halo(
            CHUNKS,
            cot_hbm.at[:, columns((1 - core) * (cols - HALO), HALO)],
            cot.at[pl.ds(1, rows), columns(side * (cols + HALO), HALO)],
            (lat, mate),
        )

    low = pl.ds(0, HALO)
    high = pl.ds(cols - HALO, HALO)
    ext_low = pl.ds(0, HALO)
    ext_mid = pl.ds(HALO, cols)
    ext_high = pl.ds(cols + HALO, HALO)
    first, last = pl.ds(0, 1), pl.ds(rows - 1, 1)
    above, below = pl.ds(0, 1), pl.ds(rows + 1, 1)
    down = [
        halo(5, cot_hbm.at[last, high], cot.at[above, ext_low], (lat + 1, east)),
        halo(6, cot_hbm.at[last, low], cot.at[above, ext_high], (lat + 1, west)),
        halo(7, cot_hbm.at[last], cot.at[above, ext_mid], (lat + 1, lon)),
    ]
    up = [
        halo(8, cot_hbm.at[first, high], cot.at[below, ext_low], (lat - 1, east)),
        halo(9, cot_hbm.at[first, low], cot.at[below, ext_high], (lat - 1, west)),
        halo(10, cot_hbm.at[first], cot.at[below, ext_mid], (lat - 1, lon)),
    ]

    @pl.when(has_down)
    def _():
        for copy in down:
            copy.start()

    @pl.when(has_up)
    def _():
        for copy in up:
            copy.start()

    near_copy(False).start()
    for chunk in range(CHUNKS):
        far_copy(chunk, False).start()

    latitude = lax.broadcasted_iota(jnp.int32, area.shape, 0) + (lat * rows - 1)
    area[...] = (math.pi / 2) * jnp.sin(math.pi * (latitude.astype(F32) + 0.5) / nlat)

    for load in loads[:3]:
        load.wait()
    size = 2 * HALO + 1
    tap_in = lax.broadcasted_iota(jnp.int32, (size, 128), 0)
    tap_out = lax.broadcasted_iota(jnp.int32, (size, 128), 1)
    reverse = jnp.where(tap_in + tap_out == 2 * HALO, 1.0, 0.0).astype(BF16)
    offset = jnp.abs(lax.broadcasted_iota(jnp.int32, (size, nlat), 0) - HALO)
    inside = offset <= width[...]
    for r in range(3):
        which = jnp.where(inside, index[r], K).astype(F32).astype(BF16)
        flip_v[r] = dot(values[r], reverse, ((0,), (0,)))
        flip_i[r] = dot(which, reverse, ((0,), (0,)))

    def clip_row(row):
        return jnp.clip(lat * rows + row - 1, 0, nlat - 1)

    @pl.loop(0, rows, unroll=8)
    def _(row):
        vals = jnp.zeros((WINDOW, 256), F32)
        which = jnp.zeros((WINDOW, 256), F32)
        rest = jnp.zeros((WINDOW, 128), F32)
        for t in range(3):
            at = pl.ds(clip_row(row + t), 1)
            spots = [
                jnp.concatenate(
                    [jnp.broadcast_to(table[2 - t, at, :], (WINDOW, 128)), rest], axis=1
                )
                for table in (flip_v, flip_i)
            ]
            spots = [pltpu.roll(x, REACH * t, 1, stride=1, stride_axis=0) for x in spots]
            vals += spots[0]
            which += spots[1]
        vals = vals.astype(BF16)
        which = which.astype(BF16)
        for k in range(K):
            taps[row, k * WINDOW : (k + 1) * WINDOW] = jnp.where(
                which == BF16(k), vals, jnp.zeros_like(vals)
            )

    def scale_row(row, at):
        factor = area[pl.ds(row, 1), :]
        factor = jnp.concatenate([factor] * (chans // 128), axis=1)
        cot[row, at] = (cot[row, at].astype(F32) * factor).astype(BF16)

    def scale_edge(row):
        scale_row(row, pl.ds(0, cols + 2 * HALO))

    loads[3].wait()
    pl.loop(1, rows + 1, unroll=4)(lambda row: scale_row(row, ext_mid))

    def filter_rows(side, start, stop):
        for row in range(start, stop):
            lhs = taps[row][:, :DEPTH]
            for u in range(side_cols // WINDOW):
                at = pl.ds(pl.multiple_of(side * side_cols + u * WINDOW, WINDOW), REACH)
                rhs = cot[row : row + 3, at].reshape(DEPTH, chans)
                result = dot(lhs, rhs, ((1,), (0,))).astype(BF16)
                to = row * side_cols + u * WINDOW
                for k in range(K):
                    spread[side, k, to : to + WINDOW] = result[k * WINDOW : (k + 1) * WINDOW]

    def field_product(side, k, start, stop):
        lhs = field[side, start:stop].reshape((stop - start) * side_cols, chans)
        rhs = spread[side, k, start * side_cols : stop * side_cols]
        return dot(lhs, rhs, ((0,), (0,)))

    def add_product(k, start, stop):
        result = field_product(far, k, start, stop)
        part[0, k] += result[:, :lanes]
        part[1, k] += result[:, lanes:]

    near_copy(True).wait_recv()
    near_at = columns(near * (cols + HALO), HALO)
    pl.loop(1, rows + 1, unroll=4)(lambda row: scale_row(row, near_at))
    filter_rows(near, 1, rows - 1)

    loads[4].wait()
    loads[5].wait()
    for k in range(K):
        result = field_product(near, k, 1, rows - 1)
        part[0, k] = result[:, :lanes]
        part[1, k] = result[:, lanes:]

    far_at = columns(far * (cols + HALO), HALO)
    for chunk in range(CHUNKS):
        if chunk == CHUNKS - 1:
            for k in range(K):
                add_product(k, 1, rows // 2)
        far_copy(chunk, True).wait_recv()
        for row in range(1 + chunk * tall, 1 + (chunk + 1) * tall):
            scale_row(row, far_at)
        start = max(chunk * tall - 1, 1)
        stop = (chunk + 1) * tall - 1
        filter_rows(far, start, stop)

    @pl.when(has_up)
    def _():
        for copy in down:
            copy.wait_recv()

    @pl.when(has_down)
    def _():
        for copy in up:
            copy.wait_recv()

    @pl.when(jnp.logical_not(has_up))
    def _():
        cot[0] = jnp.zeros_like(cot[0])

    @pl.when(jnp.logical_not(has_down))
    def _():
        cot[rows + 1] = jnp.zeros_like(cot[rows + 1])

    scale_edge(0)
    scale_edge(rows + 1)
    for side in range(2):
        filter_rows(side, 0, 1)
        filter_rows(side, rows - 1, rows)

    def add_edges(k):
        ends = (0, rows - 1)
        lhs = jnp.concatenate([field[side, row] for side in range(2) for row in ends], axis=0)
        rhs = jnp.concatenate(
            [
                spread[side, k, row * side_cols : (row + 1) * side_cols]
                for side in range(2)
                for row in ends
            ],
            axis=0,
        )
        result = dot(lhs, rhs, ((0,), (0,)))
        part[0, k] += result[:, :lanes]
        part[1, k] += result[:, lanes:]

    def pair_copy(group):
        ks = pl.ds(group * GROUP, GROUP)
        return pltpu.make_async_remote_copy(
            src_ref=part.at[1 - core, ks], dst_ref=pair.at[ks],
            send_sem=pair_send.at[group], recv_sem=pair_recv.at[group],
            device_id=(lat, mate), device_id_type=MESH,
        )

    def lat_copy(group, step):
        ks = pl.ds(group * GROUP, GROUP)
        peer = lax.rem(lat + step, n_lat)
        return pltpu.make_async_remote_copy(
            src_ref=half.at[ks, pl.ds(pl.multiple_of(peer * wide, wide), wide)],
            dst_ref=lat_in.at[step, ks],
            send_sem=lat_send.at[group, step], recv_sem=lat_recv.at[group, step],
            device_id=(peer, lon), device_id_type=MESH,
        )

    def lon_copy(k, half_ring):
        owner = half_ring * ring + k % ring
        return owner, pltpu.make_async_remote_copy(
            src_ref=band.at[k], dst_ref=lon_in.at[k // ring, chip],
            send_sem=lon_send.at[k, half_ring], recv_sem=lon_recv.at[k // ring, chip],
            device_id=(lat, owner * 2 + core), device_id_type=MESH,
        )

    def lon_arrival(k, source):
        return pltpu.make_async_remote_copy(
            src_ref=band.at[k], dst_ref=lon_in.at[k // ring, source],
            send_sem=lon_send.at[k, 0], recv_sem=lon_recv.at[k // ring, source],
            device_id=(lat, source * 2 + core), device_id_type=MESH,
        )

    def reduce_pair(group):
        pair_copy(group).wait_recv()
        for k in range(group * GROUP, (group + 1) * GROUP):
            half[k] = (part[core, k] + pair[k]).astype(BF16)

        @pl.loop(1, n_lat)
        def _(step):
            lat_copy(group, step).start()

    def reduce_lat(group):
        @pl.loop(1, n_lat)
        def _(step):
            lat_copy(group, step).wait_recv()

        at = pl.ds(pl.multiple_of(lat * wide, wide), wide)
        for k in range(group * GROUP, (group + 1) * GROUP):
            total = half[k, at].astype(F32)
            for step in range(1, n_lat):
                total += lat_in[step, k].astype(F32)
            band[k] = total.astype(BF16)
            for half_ring in range(2):
                owner, copy = lon_copy(k, half_ring)
                pl.when(chip != owner)(copy.start)

    for group in range(GROUPS):
        for k in range(group * GROUP, (group + 1) * GROUP):
            add_product(k, rows // 2, rows - 1)
            add_edges(k)
        pair_copy(group).start()

    loads[6].wait()

    def grad_block(side, block):
        at = pl.ds(block * 256, 256)
        total = dot(spread[side, 0, at], weight[0], ((1,), (1,)))
        for k in range(1, K):
            total += dot(spread[side, k, at], weight[k], ((1,), (1,)))
        high = 256 // side_cols
        to = pl.ds(block * high, high)
        grad_ref[to, side * side_cols : (side + 1) * side_cols] = total.reshape(
            high, side_cols, chans
        )

    blocks = [(side, block) for side in range(2) for block in range(side_spots // 256)]
    cuts = [len(blocks) * n // 8 for n in (0, 2, 3, 4, 8)]
    for step in range(4):
        for block in blocks[cuts[step] : cuts[step + 1]]:
            grad_block(*block)
        if step < GROUPS:
            reduce_pair(step)
    for group in range(GROUPS):
        reduce_lat(group)

    def all_copy(k, step):
        return pltpu.make_async_remote_copy(
            src_ref=final.at[core, k], dst_ref=final.at[core, k],
            send_sem=all_send.at[k // ring, step], recv_sem=all_recv.at[core, k],
            device_id=(lat, base + lax.rem(lon - base + step, 2 * ring)),
            device_id_type=MESH,
        )

    def all_arrival(k, half_core):
        return pltpu.make_async_remote_copy(
            src_ref=final.at[half_core, k], dst_ref=final.at[half_core, k],
            send_sem=all_send.at[0, 0], recv_sem=all_recv.at[half_core, k],
            device_id=(lat, base + 2 * (k % ring) + half_core), device_id_type=MESH,
        )

    for k in range(K):
        @pl.when(spot == k % ring)
        def _():
            @pl.loop(1, chips)
            def _(step):
                lon_arrival(k, lax.rem(chip + step, chips)).wait_recv()

            total = band[k].astype(F32)
            for step in range(1, chips):
                total += lon_in[k // ring, lax.rem(chip + step, chips)].astype(F32)
            final[core, k] = (total * scale).astype(BF16)

            @pl.loop(1, 2 * ring)
            def _(step):
                all_copy(k, step).start()

    for k in range(K):
        for half_core in range(2):
            @pl.when(jnp.logical_or(spot != k % ring, core != half_core))
            def _():
                all_arrival(k, half_core).wait_recv()

            of_core = slice(half_core * lanes, (half_core + 1) * lanes)
            wgrad_ref[k, :, of_core] = final[half_core, k].astype(F32)

    near_copy(False).wait_send()
    for chunk in range(CHUNKS):
        far_copy(chunk, False).wait_send()

    @pl.when(has_down)
    def _():
        for copy in down:
            copy.wait_send()

    @pl.when(has_up)
    def _():
        for copy in up:
            copy.wait_send()

    for group in range(GROUPS):
        pair_copy(group).wait_send()

        @pl.loop(1, n_lat)
        def _(step):
            lat_copy(group, step).wait_send()

    for k in range(K):
        for half_ring in range(2):
            owner, copy = lon_copy(k, half_ring)
            pl.when(chip != owner)(copy.wait_send)

        @pl.when(spot == k % ring)
        def _():
            @pl.loop(1, 2 * ring)
            def _(step):
                all_copy(k, step).wait_send()


def write_kernel(grad_ref, wgrad_ref, grad_hbm, wgrad_hbm, sems):
    pieces = sems.shape[0] - 1
    tall = grad_ref.shape[0] // pieces
    copies = [pltpu.make_async_copy(wgrad_ref, wgrad_hbm, sems.at[pieces])]
    for piece in range(pieces):
        at = pl.ds(piece * tall, tall)
        copies.append(pltpu.make_async_copy(grad_ref.at[at], grad_hbm.at[at], sems.at[piece]))
    for copy in copies:
        copy.start()
    for copy in copies:
        copy.wait()


def write_out(grad, wgrad):
    vmem = pl.BlockSpec(memory_space=pltpu.VMEM)
    whole = pl.BlockSpec(memory_space=pltpu.HBM)
    return pl.pallas_call(
        write_kernel,
        out_shape=tuple(jax.ShapeDtypeStruct(x.shape, x.dtype) for x in (grad, wgrad)),
        in_specs=(vmem, vmem),
        out_specs=(whole, whole),
        scratch_shapes=[pltpu.SemaphoreType.DMA((5,))],
        compiler_params=pltpu.CompilerParams(vmem_limit_bytes=8 * 2**20),
    )(*(pltpu.with_memory_space_constraint(x, pltpu.VMEM) for x in (grad, wgrad)))


def shards(input_field, cotangent, weight, basis_values, basis_index, halo_width):
    n_lat = lax.axis_size("lat")
    n_lon = lax.axis_size("lon")
    rows, cols, chans = input_field.shape
    nlat = rows * n_lat
    chips = n_lon // 2
    wide = chans // n_lat
    lanes = chans // 2
    ring = chips // 2
    held = -(-K // ring)
    side_cols = cols // 2
    ext = cols + 2 * HALO
    size = 2 * HALO + 1
    scale = 1.0 / math.sqrt(nlat * cols * n_lon)
    sizes = (n_lat, n_lon, rows, cols, chans, nlat, scale)
    whole = pl.BlockSpec(memory_space=pltpu.HBM)
    vmem = pl.BlockSpec(memory_space=pltpu.VMEM)
    dma = pltpu.SemaphoreType.DMA
    table = pltpu.VMEM((3, nlat, 128), F32)
    grad, wgrad = pl.pallas_call(
        functools.partial(kernel, sizes),
        out_shape=(
            pltpu.VMEM((rows, cols, chans), F32),
            pltpu.VMEM((K, wide, chans), F32),
        ),
        in_specs=[whole] * 6,
        out_specs=(vmem, vmem),
        scratch_shapes=[
            pltpu.VMEM((rows + 2, ext, chans), BF16),
            pltpu.VMEM((2, rows, side_cols, chans), BF16),
            pltpu.VMEM((K, chans, chans), BF16),
            pltpu.VMEM((3, size, nlat), BF16),
            pltpu.VMEM((3, size, nlat), jnp.int32),
            pltpu.VMEM((1, nlat), jnp.int32),
            table, table,
            pltpu.VMEM((-(-(rows + 2) // 8) * 8, 128), F32),
            pltpu.VMEM((rows, K * WINDOW, 256), BF16),
            pltpu.VMEM((2, K, rows * side_cols, chans), BF16),
            pltpu.VMEM((2, K, chans, lanes), F32),
            pltpu.VMEM((K, chans, lanes), F32),
            pltpu.VMEM((K, chans, lanes), BF16),
            pltpu.VMEM((n_lat, K, wide, lanes), BF16),
            pltpu.VMEM((K, wide, lanes), BF16),
            pltpu.VMEM((held, chips, wide, lanes), BF16),
            pltpu.VMEM((2, K, wide, lanes), BF16),
            dma((7,)), dma((11,)), dma((11,)), dma((GROUPS,)), dma((GROUPS,)),
            dma((GROUPS, n_lat)), dma((GROUPS, n_lat)), dma((K, 2)), dma((held, chips)),
            dma((held, 2 * ring)), dma((2, K)),
        ],
        compiler_params=pltpu.CompilerParams(
            collective_id=0, has_side_effects=True, vmem_limit_bytes=40 * 2**20
        ),
        cost_estimate=pl.CostEstimate(
            flops=2 * K * rows * cols * chans * (3 * ext + 2 * chans),
            bytes_accessed=6 * 2**20, transcendentals=0,
        ),
    )(
        *(
            pltpu.with_memory_space_constraint(x, pltpu.HBM) for x in (
            cotangent, input_field, weight,
            basis_values.transpose(1, 2, 0), basis_index.transpose(1, 2, 0),
            halo_width.reshape(1, nlat),
        )),
    )
    return write_out(grad, wgrad)


def solution(mesh):
    in_specs = (P("lat", "lon", None), P("lat", "lon", None), P(), P(), P(), P())
    out_specs = (P("lat", "lon", None), P(None, "lat", None))
    return jax.shard_map(shards, mesh=mesh, in_specs=in_specs, out_specs=out_specs, check_vma=False)
```
